256 devices in a mesh: chan: 32 (over z, x_hi, core), tm: 8 (over y, x_lo).
Axes of the slice: x: 4 (x_hi: 2, x_lo: 2; x = x_hi * 2 + x_lo), y: 4, z: 8, core: 2. Of those that a mesh axis runs over, the one named last changes fastest.
Arguments:
- spectra: bfloat16 [2048, 32, 2048], P('chan', 'tm'), may hold values from -400 to 400
- positions: int32 [2048], replicated, may hold values from 0 to 3070, as said below
- source_order: int32 [32], replicated, may hold values from 0 to 31, each once
Outputs:
- correlations: float32 [128, 2048], P('chan')
The draws below stay inside these ranges and needn't reach their ends.
Inputs may be any that keep to these rules, and one draw needn't show every extreme that they name: positions start at 0 and rise by 1 or 2 from each channel to the next; exactly (2047) // 2 of the rises are 2. `source_order`: each block appears once.
All inputs are finite; a program needn't handle non-finite values.
Results may differ from the reference program's by a relative error of at most 0.005.
Values may be sent and summed in bfloat16 or wider, within the bound.
A program may use at most 64 MiB of HBM per device.

```python
import jax
import jax.numpy as jnp
from jax import lax

SRC = 64
FREQ = 1024
SEG_DEV = 4
STEPS = 2
LAGS = 2048
SENSOR_TRACES = 2048
RECORD_WINDOWS = 32
BINS = 128
NBLK = 32
N_TM = 8


def draw_spectra(key, part):
    key = jax.random.fold_in(key, 11)
    first, second, third, quarter_portion = jax.random.split(key, 4)
    starting_distance = jnp.clip(jax.random.normal(first, (SENSOR_TRACES, RECORD_WINDOWS, 2 * FREQ), jnp.float32), -4.0, 4.0)
    reach = jnp.log(10.0)
    trace_multiplier = jnp.exp(jax.random.uniform(second, (SENSOR_TRACES, 1, 1), jnp.float32) * reach)
    spectral_multiplier = jnp.exp(jax.random.uniform(third, (1, 1, FREQ), jnp.float32) * reach)
    spectral_multiplier = jnp.concatenate([spectral_multiplier, spectral_multiplier], 2)
    packet_extent = jnp.exp(jax.random.uniform(quarter_portion, (SENSOR_TRACES, RECORD_WINDOWS, 1), jnp.float32) * jnp.log(10.0))
    return (starting_distance * trace_multiplier * spectral_multiplier * packet_extent * 0.09).astype(jnp.bfloat16)


def draw_positions(key, part):
    key = jax.random.fold_in(key, 23)
    order = jax.random.permutation(key, SENSOR_TRACES - 1).astype(jnp.int32)
    spacing = jnp.where(order < (SENSOR_TRACES - 1) // 2, 2, 1).astype(jnp.int32)
    rises = jnp.cumsum(spacing).astype(jnp.int32)
    return jnp.concatenate([jnp.zeros((1,), jnp.int32), rises]).astype(jnp.int32)


def setup_inputs(seed: int = 0) -> dict:
    key_list = jax.random.split(jax.random.key(seed), 4)
    return {
        "spectra": draw_spectra(jax.random.fold_in(key_list[3], 71), 0),
        "positions": draw_positions(jax.random.fold_in(key_list[3], 71), 0),
        "source_order": jax.random.permutation(key_list[2], NBLK).astype(jnp.int32),
    }


water_level = 0.1
pair_eps = 1e-06
block_rows = 8

def lag_tables():
    freq_ids = jnp.arange(FREQ, dtype=jnp.int32)
    shifts = jnp.arange(LAGS, dtype=jnp.int32) - FREQ
    phase = freq_ids[:, None] * shifts[None, :] % LAGS
    angle = 2.0 * jnp.pi / LAGS * phase.astype(jnp.float32)
    return (jnp.cos(angle), jnp.sin(angle))

def reference(spectra, positions, source_order):
    data = spectra.astype(jnp.float32)
    power = lax.optimization_barrier(jnp.sum(data[..., :FREQ] ** 2 + data[..., FREQ:] ** 2, axis=1))
    inverse = 1.0 / jnp.sqrt(power / RECORD_WINDOWS + water_level)
    white = (data * jnp.concatenate([inverse, inverse], 1)[:, None, :]).astype(jnp.bfloat16)
    grouped = white.reshape(SENSOR_TRACES, N_TM, SEG_DEV, 2 * FREQ)
    all_ids = jnp.arange(SENSOR_TRACES, dtype=jnp.int32)
    loop = SENSOR_TRACES + 1 + (SENSOR_TRACES - 1) // 2
    blocks = SRC // block_rows
    stack = jnp.zeros((BINS, 2 * FREQ), jnp.float32)
    count = jnp.zeros((BINS,), jnp.float32)
    for step in range(STEPS):
        start = (source_order[step] * SRC).astype(jnp.int32)
        source = lax.dynamic_slice_in_dim(grouped, start, SRC, 0)
        source = source.reshape(blocks, block_rows, N_TM, SEG_DEV, 2 * FREQ)
        source_pos = lax.dynamic_slice_in_dim(positions, start, SRC, 0).reshape(blocks, block_rows)
        source_ids = (start + jnp.arange(SRC, dtype=jnp.int32)).reshape(blocks, block_rows)

        def one_block(total, item):
            rows, pos, ids = item
            gap = jnp.abs(pos[:, None] - positions[None, :])
            offset = jnp.minimum(gap, loop - gap)
            pair_bins = offset * (2 * BINS) // (loop + 1)
            pair_bins = jnp.where(ids[:, None] == all_ids[None, :], BINS, pair_bins).astype(jnp.int32).reshape(-1)
            for group in range(N_TM):
                src = rows[:, group].astype(jnp.float32)
                rec = grouped[:, group].astype(jnp.float32)
                sr, si = (src[..., :FREQ], src[..., FREQ:])
                rr, ri = (rec[..., :FREQ], rec[..., FREQ:])
                real = jnp.einsum('sgf,cgf->scf', sr, rr, precision=lax.Precision.HIGHEST)
                real = real + jnp.einsum('sgf,cgf->scf', si, ri, precision=lax.Precision.HIGHEST)
                imag = jnp.einsum('sgf,cgf->scf', sr, ri, precision=lax.Precision.HIGHEST)
                imag = imag - jnp.einsum('sgf,cgf->scf', si, rr, precision=lax.Precision.HIGHEST)
                cross = jnp.concatenate([real, imag], 2)
                scale = lax.rsqrt(lax.optimization_barrier(jnp.mean(cross * cross, axis=2, keepdims=True)) + pair_eps)
                normed = (cross * scale).astype(jnp.bfloat16).astype(jnp.float32).reshape(-1, 2 * FREQ)
                total = total + jax.ops.segment_sum(normed, pair_bins, num_segments=BINS + 1)[:BINS]
            ones = jnp.ones(pair_bins.shape, jnp.float32)
            return (total, jax.ops.segment_sum(ones, pair_bins, num_segments=BINS + 1)[:BINS])
        stack, counts = lax.scan(one_block, stack, (source, source_pos, source_ids))
        count = count + lax.optimization_barrier(jnp.sum(counts, axis=0))
    cos_table, sin_table = lag_tables()
    lagged = jnp.dot(stack[:, :FREQ], cos_table, precision=lax.Precision.HIGHEST)
    lagged = lagged - jnp.dot(stack[:, FREQ:], sin_table, precision=lax.Precision.HIGHEST)
    return lagged / jnp.sqrt(count * (N_TM * FREQ))[:, None]
```

```python
import functools

import jax
import jax.numpy as jnp
import numpy as np
from jax import lax
from jax.experimental import pallas as pl
from jax.experimental.pallas import tpu as pltpu
from jax.sharding import PartitionSpec as P

SRC = 64
STEPS = 2
SLOTS = 12
MIB = 1024 * 1024

water_level = 0.1
pair_eps = 1e-06
f32 = jnp.float32
bf16 = jnp.bfloat16


def to_bins(gap, loop, bins):
    offset = jnp.minimum(gap, loop - gap)
    return jnp.floor((offset * (2 * bins) + 0.5) * (1.0 / (loop + 1)))


def as_column(row):
    n = row.shape[1]
    eye = lax.broadcasted_iota(jnp.int32, (n, n), 0) == lax.broadcasted_iota(jnp.int32, (n, n), 1)
    return jnp.sum(jnp.where(eye, row, 0.0), axis=1, keepdims=True)


def corr_kernel(channels, bins, order_ref, pos_ref, w_ref, s_ref, out_ref,
                w2, s32, fs, fr, amat, hmask, wf0, wf1, t0, t1, acc):
    rows, width = w_ref.shape
    freq = width // 8
    loop = float(channels + 1 + (channels - 1) // 2)
    mine = lax.axis_index("chan")
    w2[:rows] = w_ref[...]
    w2[rows:] = w_ref[...]

    def unpack(i, _):
        r = pl.multiple_of(i * 16, 16)
        s32[pl.ds(r, 16), :] = s_ref[pl.ds(r, 16), :].astype(f32)
        return 0

    lax.fori_loop(0, STEPS * SRC // 16, unpack, 0)

    fw = fs.shape[1] // 16

    def features(x_ref, out, double, start, r):
        re = [x_ref[pl.ds(r, 16), pl.ds(pl.multiple_of(start + 2 * a * freq, fw), fw)].astype(f32)
              for a in range(4)]
        im = [x_ref[pl.ds(r, 16), pl.ds(pl.multiple_of(start + (2 * a + 1) * freq, fw), fw)].astype(f32)
              for a in range(4)]
        n = 0
        for a in range(4):
            out[pl.ds(r, 16), n * fw:(n + 1) * fw] = (re[a] * re[a] + im[a] * im[a]).astype(bf16)
            n += 1
        for a in range(4):
            for b in range(a + 1, 4):
                x = re[a] * re[b] + im[a] * im[b]
                y = re[a] * im[b] - im[a] * re[b]
                if double:
                    x, y = x + x, y + y
                out[pl.ds(r, 16), n * fw:(n + 1) * fw] = x.astype(bf16)
                out[pl.ds(r, 16), (n + 1) * fw:(n + 2) * fw] = y.astype(bf16)
                n += 2

    energy = jnp.zeros((STEPS * SRC, 2 * rows), f32)

    def add_energy(i, energy):
        start = pl.multiple_of(i * fw, fw)

        def one(j, _):
            r = pl.multiple_of(j * 16, 16)
            features(s_ref, fs, False, start, r)
            features(w2, fr, True, start, r)
            return 0

        lax.fori_loop(0, STEPS * SRC // 16, one, 0)
        return energy + lax.dot_general(fs[...], fr[...], (((1,), (1,)), ((), ())),
                                        preferred_element_type=f32)

    energy = lax.fori_loop(0, freq // fw, add_energy, energy)
    scale = lax.rsqrt(jnp.maximum(energy, 0.0) * (1.0 / (2 * freq)) + pair_eps)

    rec = pos_ref[pl.ds(mine, 1), :].astype(f32)
    lane = lax.broadcasted_iota(jnp.int32, (SRC, 2 * rows), 1)
    rec_ids = mine * rows + lane % rows
    firsts = []
    for step in range(STEPS):
        block = order_ref[step]
        src = as_column(pos_ref[pl.ds(block, 1), :].astype(f32)[:, :SRC])
        pair_bins = to_bins(jnp.abs(src - rec), loop, bins)
        src_ids = block * SRC + lax.broadcasted_iota(jnp.int32, (SRC, 2 * rows), 0)
        weight = jnp.where(src_ids == rec_ids, 0.0, scale[step * SRC:(step + 1) * SRC])
        first = jnp.min(jnp.min(pair_bins, axis=1, keepdims=True), axis=0, keepdims=True)
        firsts.append(first)
        rel = pair_bins - first
        upper = rel >= float(SLOTS)
        slot = jnp.where(upper, rel - float(SLOTS), rel)
        for k in range(SLOTS):
            here = slot == float(k)
            part = jnp.where(here, weight, 0.0)
            high = part.astype(bf16)
            low = (part - high.astype(f32)).astype(bf16)
            amat[step, k * SRC:(k + 1) * SRC, :] = jnp.where(lane < rows, high.astype(f32), low.astype(f32)).astype(bf16)
            mark = jnp.max(jnp.where(here & upper, 1.0, 0.0), axis=1, keepdims=True)
            hmask[step, k * SRC:(k + 1) * SRC, :] = jnp.broadcast_to(mark, (SRC, 128))

    chunks = freq // 128
    total = STEPS * chunks

    def project(i, wf, t):
        step, col = i // chunks, (i % chunks) * 128
        for n in range(8):
            wf[:, n * 128:(n + 1) * 128] = w2[:, pl.ds(pl.multiple_of(n * freq + col, 128), 128)]
        t[...] = jnp.dot(amat[step], wf[...], preferred_element_type=f32)

    def gather(i, t):
        step, col = i // chunks, pl.multiple_of((i % chunks) * 128, 128)
        for k in range(SLOTS):
            sums = [None] * 4
            for g in range(SRC // 8):
                r = k * SRC + g * 8
                row = pl.multiple_of(step * SRC + g * 8, 8)
                re, im = [], []
                for a in range(4):
                    tr = t[r:r + 8, 2 * a * 128:(2 * a + 1) * 128]
                    ti = t[r:r + 8, (2 * a + 1) * 128:(2 * a + 2) * 128]
                    sr = s32[pl.ds(row, 8), pl.ds(pl.multiple_of(2 * a * freq + col, 128), 128)]
                    si = s32[pl.ds(row, 8), pl.ds(pl.multiple_of((2 * a + 1) * freq + col, 128), 128)]
                    re += [sr * tr, si * ti]
                    im.append(sr * ti - si * tr)
                real = ((re[0] + re[1]) + (re[2] + re[3])) + ((re[4] + re[5]) + (re[6] + re[7]))
                imag = (im[0] + im[1]) + (im[2] + im[3])
                mark = hmask[step, r:r + 8, :]
                new = [real, imag, real * mark, imag * mark]
                sums = new if g == 0 else [x + y for x, y in zip(sums, new)]
            base = step * (2 * SLOTS * 8)
            acc[pl.ds(pl.multiple_of(base + k * 8, 8), 8), pl.ds(col, 128)] = sums[0]
            acc[pl.ds(pl.multiple_of(base + k * 8, 8), 8), pl.ds(pl.multiple_of(freq + col, 128), 128)] = sums[1]
            base = base + SLOTS * 8
            acc[pl.ds(pl.multiple_of(base + k * 8, 8), 8), pl.ds(col, 128)] = sums[2]
            acc[pl.ds(pl.multiple_of(base + k * 8, 8), 8), pl.ds(pl.multiple_of(freq + col, 128), 128)] = sums[3]

    project(0, wf0, t0)

    def pair(j, _):
        project(2 * j + 1, wf1, t1)
        gather(2 * j, t0)
        project(jnp.minimum(2 * j + 2, total - 1), wf0, t0)
        gather(2 * j + 1, t1)
        return 0

    lax.fori_loop(0, total // 2, pair, 0)

    span = 2 * SLOTS * 8
    col = lax.broadcasted_iota(jnp.int32, (bins, span), 1)
    row = lax.broadcasted_iota(jnp.int32, (bins, span), 0).astype(f32)
    marked = col >= SLOTS * 8
    k = ((col - jnp.where(marked, SLOTS * 8, 0)) // 8).astype(f32)
    place = []
    for step in range(STEPS):
        at = row == firsts[step] + k
        above = row == firsts[step] + k + float(SLOTS)
        place.append(jnp.where(marked, jnp.where(above, 1.0, 0.0) - jnp.where(at, 1.0, 0.0),
                               jnp.where(at, 1.0, 0.0)).astype(bf16))
    for c in range(0, width // 4, 256):
        out = jnp.zeros((bins, 256), f32)
        for step in range(STEPS):
            value = acc[step * span:(step + 1) * span, c:c + 256]
            high = value.astype(bf16)
            low = (value - high.astype(f32)).astype(bf16)
            out += jnp.dot(place[step], high, preferred_element_type=f32)
            out += jnp.dot(place[step], low, preferred_element_type=f32)
        out_ref[:, c:c + 256] = out


def correlate(white, sources, pos2, order, bins):
    rows, width = white.shape
    freq = width // 8
    sources_n = sources.shape[0]
    fw = 256
    vm = pl.BlockSpec(memory_space=pltpu.VMEM)
    return pl.pallas_call(
        functools.partial(corr_kernel, pos2.shape[0] * rows, bins),
        out_shape=jax.ShapeDtypeStruct((bins, 2 * freq), f32),
        in_specs=[pl.BlockSpec(memory_space=pltpu.SMEM), vm, vm, vm],
        out_specs=vm,
        scratch_shapes=[
            pltpu.VMEM((2 * rows, width), bf16),
            pltpu.VMEM((sources_n, width), f32),
            pltpu.VMEM((sources_n, 16 * fw), bf16),
            pltpu.VMEM((2 * rows, 16 * fw), bf16),
            pltpu.VMEM((STEPS, SLOTS * SRC, 2 * rows), bf16),
            pltpu.VMEM((STEPS, SLOTS * SRC, 128), f32),
            pltpu.VMEM((2 * rows, 1024), bf16),
            pltpu.VMEM((2 * rows, 1024), bf16),
            pltpu.VMEM((SLOTS * SRC, 1024), f32),
            pltpu.VMEM((SLOTS * SRC, 1024), f32),
            pltpu.VMEM((STEPS * 2 * SLOTS * 8, 2 * freq), f32),
        ],
        compiler_params=pltpu.CompilerParams(vmem_limit_bytes=56 * MIB),
        name="correlate",
    )(order, pos2, white, sources)


BIN_DEV = 4


def power_kernel(n_tm, x_ref, w_ref, part, got, inv, send1, recv1, send2, recv2):
    rows, width = x_ref.shape
    freq = width // 8
    cols = freq // n_tm
    me = lax.axis_index("tm")
    peers = [lax.rem(me + d, n_tm) for d in range(1, n_tm)]
    barrier = pltpu.get_barrier_semaphore()
    for peer in peers:
        pl.semaphore_signal(barrier, inc=1, device_id={"tm": peer})
    for p in range(n_tm):
        total = None
        for n in range(8):
            v = x_ref[:, n * freq + p * cols:n * freq + (p + 1) * cols].astype(f32)
            total = v * v if total is None else total + v * v
        part[p] = total.astype(bf16)
    pl.semaphore_wait(barrier, n_tm - 1)

    def exchange(src, dst, send, recv, d):
        return pltpu.make_async_remote_copy(src_ref=src, dst_ref=dst, send_sem=send, recv_sem=recv,
                                            device_id={"tm": peers[d - 1]})

    copies = [exchange(part.at[peers[d - 1]], got.at[me], send1.at[d], recv1.at[me], d) for d in range(1, n_tm)]
    for copy in copies:
        copy.start()
    total = part[me].astype(f32)
    for d in range(1, n_tm):
        other = lax.rem(me - d + n_tm, n_tm)
        exchange(part.at[me], got.at[other], send1.at[d], recv1.at[other], d).wait_recv()
        total = total + got[other].astype(f32)
    inv[me] = 1.0 / jnp.sqrt(total * (1.0 / (4 * n_tm)) + water_level)
    second = [exchange(inv.at[me], inv.at[me], send2.at[d], recv2.at[me], d) for d in range(1, n_tm)]
    for copy in second:
        copy.start()

    def whiten(p):
        factor = inv[p]
        for n in range(8):
            at = pl.ds(pl.multiple_of(n * freq + p * cols, cols), cols)
            w_ref[:, at] = (x_ref[:, at].astype(f32) * factor).astype(bf16)

    whiten(me)
    for d in range(1, n_tm):
        other = lax.rem(me - d + n_tm, n_tm)
        exchange(inv.at[me], inv.at[other], send2.at[d], recv2.at[other], d).wait_recv()
        whiten(other)
    for copy in copies + second:
        copy.wait_send()


def whiten(flat, n_tm):
    rows, width = flat.shape
    cols = width // 8 // n_tm
    vm = pl.BlockSpec(memory_space=pltpu.VMEM)
    return pl.pallas_call(
        functools.partial(power_kernel, n_tm),
        out_shape=jax.ShapeDtypeStruct((rows, width), bf16),
        in_specs=[vm],
        out_specs=vm,
        scratch_shapes=[
            pltpu.VMEM((n_tm, rows, cols), bf16),
            pltpu.VMEM((n_tm, rows, cols), bf16),
            pltpu.VMEM((n_tm, rows, cols), f32),
            pltpu.SemaphoreType.DMA((n_tm,)),
            pltpu.SemaphoreType.DMA((n_tm,)),
            pltpu.SemaphoreType.DMA((n_tm,)),
            pltpu.SemaphoreType.DMA((n_tm,)),
        ],
        compiler_params=pltpu.CompilerParams(collective_id=0, has_side_effects=True, vmem_limit_bytes=32 * MIB),
        name="whiten",
    )(flat)


def reduce_kernel(n_chan, n_tm, channels, bins, order_ref, pos_ref, stack_ref, table_ref, out_ref,
                  table, out0, got0, out1, got1, out2, got2, parts, xk,
                  table_sem, sem0, send1, recv1, send2, recv2, send3, recv3):
    width = stack_ref.shape[1]
    freq = width // 2
    loop = float(channels + 1 + (channels - 1) // 2)
    me_c, me_t = lax.axis_index("chan"), lax.axis_index("tm")
    zh, core = me_c // 2, lax.rem(me_c, 2)
    n_zh = n_chan // 2
    cols = freq // n_tm
    sibling = zh * 2 + 1 - core
    tms = [lax.rem(me_t + d, n_tm) for d in range(n_tm)]
    zhs = [lax.rem(zh + d, n_zh) for d in range(n_zh)]
    group = [(me_c, core, tms[d]) for d in range(1, n_tm)] + [(sibling, 1 - core, tms[d]) for d in range(n_tm)]
    back = [lax.rem(me_t - d + n_tm, n_tm) for d in range(n_tm)]
    group_back = [(core, back[d]) for d in range(1, n_tm)] + [(1 - core, back[d]) for d in range(n_tm)]
    barrier = pltpu.get_barrier_semaphore()
    for chan, _, tm in group:
        pl.semaphore_signal(barrier, inc=1, device_id={"chan": chan, "tm": tm})
    for q in zhs[1:]:
        pl.semaphore_signal(barrier, inc=1, device_id={"chan": q * 2 + core, "tm": me_t})
    load = pltpu.make_async_copy(table_ref, table, table_sem.at[0])
    load.start()

    def remote(src, dst, send, recv, chan, tm):
        return pltpu.make_async_remote_copy(src_ref=src, dst_ref=dst, send_sem=send, recv_sem=recv,
                                            device_id={"chan": chan, "tm": tm})

    out0[...] = stack_ref[:, pl.ds(pl.multiple_of((1 - core) * freq, freq), freq)].astype(bf16)
    pl.semaphore_wait(barrier, len(group) + n_zh - 1)
    swap = remote(out0, got0, sem0.at[0], sem0.at[1], sibling, me_t)
    swap.start()

    counts = []
    for step in range(STEPS):
        src = as_column(pos_ref[pl.ds(order_ref[step], 1), :].astype(f32)[:, :SRC])

        def count(i, sums):
            pair_bins = to_bins(jnp.abs(src - pos_ref[pl.ds(i, 1), :].astype(f32)), loop, bins)
            rel = pair_bins - (me_c * BIN_DEV).astype(f32)
            return tuple(s + jnp.where(rel == float(b), 0.5, 0.0) for b, s in enumerate(sums))

        init = tuple(jnp.zeros((SRC, pos_ref.shape[1]), f32) for _ in range(BIN_DEV))
        counts.append(lax.fori_loop(0, pos_ref.shape[0], count, init))
    factors = []
    for b in range(BIN_DEV):
        amount = sum(c[b] for c in counts)
        amount = jnp.sum(jnp.sum(amount, axis=1, keepdims=True), axis=0, keepdims=True)
        own = jnp.where(me_c * BIN_DEV + b == 0, float(STEPS * SRC), 0.0)
        factors.append(lax.rsqrt((amount - own) * float(n_tm * freq)))
    factor = jnp.concatenate(factors, 0)

    swap.wait()
    for p in range(n_tm):
        at = pl.ds(pl.multiple_of(core * freq + p * cols, cols), cols)
        out1[p] = (stack_ref[:, at] + got0[:, p * cols:(p + 1) * cols].astype(f32)).astype(bf16)
    first = [remote(out1.at[tms[d]], got1.at[me_t], send1.at[d], recv1.at[me_t], me_c, tms[d])
             for d in range(1, n_tm)]
    for copy in first:
        copy.start()
    total = out1[me_t].astype(f32)
    for d in range(1, n_tm):
        remote(out1.at[me_t], got1.at[back[d]], send1.at[d], recv1.at[back[d]], me_c, tms[d]).wait_recv()
        total = total + got1[back[d]].astype(f32)
    out2[...] = total.reshape(out2.shape)
    second = [remote(out2.at[zhs[d]], got2.at[zh], send2.at[d], recv2.at[zh], zhs[d] * 2 + core, me_t)
              for d in range(1, n_zh)]
    for copy in second:
        copy.start()
    total = out2[zh]
    for d in range(1, n_zh):
        other = lax.rem(zh - d + n_zh, n_zh)
        remote(out2.at[zh], got2.at[other], send2.at[d], recv2.at[other], zhs[d] * 2 + core, me_t).wait_recv()
        total = total + got2[other]
    slot = core * n_tm + me_t
    parts[slot] = total
    third = [remote(parts.at[slot], parts.at[slot], send3.at[i], recv3.at[slot], chan, tm)
             for i, (chan, _, tm) in enumerate(group)]
    for copy in third:
        copy.start()
    for i, ((chan, _, tm), (c, t)) in enumerate(zip(group, group_back)):
        other = c * n_tm + t
        remote(parts.at[slot], parts.at[other], send3.at[i], recv3.at[other], chan, tm).wait_recv()
    for n in range(2 * n_tm):
        value = parts[n]
        high = value.astype(bf16).astype(f32)
        xk[:, n * cols:(n + 1) * cols] = jnp.concatenate([high, value - high], 0).astype(bf16)
    load.wait()
    piece = 512
    for c in range(0, width, piece):
        both = jnp.dot(xk[...], table[:, c:c + piece], preferred_element_type=f32)
        both = both[:8] + both[8:]
        out_ref[:, c:c + piece] = jnp.where(core == 0, both[:BIN_DEV], both[BIN_DEV:]) * factor
    for copy in first + second + third:
        copy.wait_send()


def lag_table(freq):
    width = 2 * freq
    phase = np.outer(np.arange(freq), np.arange(width) - freq) % width
    angle = 2.0 * np.pi / width * phase
    return np.concatenate([np.cos(angle), -np.sin(angle)], 0).astype(jnp.bfloat16)


def reduce_stack(stack, pos2, order, n_chan, n_tm, channels):
    bins, width = stack.shape
    cols = width // 2 // n_tm
    n_zh = n_chan // 2
    vm = pl.BlockSpec(memory_space=pltpu.VMEM)
    dma = pltpu.SemaphoreType.DMA
    return pl.pallas_call(
        functools.partial(reduce_kernel, n_chan, n_tm, channels, bins),
        out_shape=jax.ShapeDtypeStruct((BIN_DEV, width), f32),
        in_specs=[pl.BlockSpec(memory_space=pltpu.SMEM), vm, vm, pl.BlockSpec(memory_space=pl.ANY)],
        out_specs=vm,
        scratch_shapes=[
            pltpu.VMEM((width, width), bf16),
            pltpu.VMEM((bins, width // 2), bf16),
            pltpu.VMEM((bins, width // 2), bf16),
            pltpu.VMEM((n_tm, bins, cols), bf16),
            pltpu.VMEM((n_tm, bins, cols), bf16),
            pltpu.VMEM((n_zh, bins // n_zh, cols), f32),
            pltpu.VMEM((n_zh, bins // n_zh, cols), f32),
            pltpu.VMEM((2 * n_tm, bins // n_zh, cols), f32),
            pltpu.VMEM((16, width), bf16),
            dma((1,)), dma((2,)), dma((n_tm,)), dma((n_tm,)), dma((n_zh,)), dma((n_zh,)),
            dma((2 * n_tm,)), dma((2 * n_tm,)),
        ],
        compiler_params=pltpu.CompilerParams(collective_id=1, has_side_effects=True, vmem_limit_bytes=48 * MIB),
        name="reduce_stack",
    )(order, pos2, stack, jnp.asarray(lag_table(width // 2)))


def local(spectra, positions, source_order):
    rows, seg_dev, width = spectra.shape
    n_chan = lax.axis_size("chan")
    n_tm = lax.axis_size("tm")
    bins = BIN_DEV * n_chan
    channels = n_chan * rows
    mine = lax.axis_index("chan")
    flat = spectra.reshape(rows, seg_dev * width)
    white = whiten(flat, n_tm)
    pos2 = positions.reshape(n_chan, rows)
    pos2 = jnp.concatenate([pos2, pos2], 1)
    sources = []
    for step in range(STEPS):
        kept = jnp.where(mine == source_order[step], white, 0).astype(bf16)
        sources.append(lax.psum(kept, "chan"))
    stack = correlate(white, jnp.concatenate(sources, 0), pos2, source_order, bins)
    return reduce_stack(stack, pos2, source_order, n_chan, n_tm, channels)


def solution(mesh):
    return jax.shard_map(
        local,
        mesh=mesh,
        in_specs=(P("chan", "tm", None), P(), P()),
        out_specs=P("chan", None),
        check_vma=False,
    )
```

```python
import functools

import jax
import jax.numpy as jnp
import numpy as np
from jax import lax
from jax.experimental import pallas as pl
from jax.experimental.pallas import tpu as pltpu
from jax.sharding import PartitionSpec as P

SRC = 64
STEPS = 2
SLOTS = 12
MIB = 1024 * 1024

water_level = 0.1
pair_eps = 1e-06
f32 = jnp.float32
bf16 = jnp.bfloat16


def to_bins(gap, loop, bins):
    offset = jnp.minimum(gap, loop - gap)
    return jnp.floor((offset * (2 * bins) + 0.5) * (1.0 / (loop + 1)))


def as_column(row):
    n = row.shape[1]
    eye = lax.broadcasted_iota(jnp.int32, (n, n), 0) == lax.broadcasted_iota(jnp.int32, (n, n), 1)
    return jnp.sum(jnp.where(eye, row, 0.0), axis=1, keepdims=True)


def corr_kernel(channels, bins, order_ref, pos_ref, w_ref, s_ref, out_ref,
                w2, s32, fs, fr, amat, hmask, wf0, wf1, t0, t1, acc):
    rows, width = w_ref.shape
    freq = width // 8
    loop = float(channels + 1 + (channels - 1) // 2)
    mine = lax.axis_index("chan")
    w2[:rows] = w_ref[...]
    w2[rows:] = w_ref[...]

    def features(x, out, double, r):
        re, im = x[0::2], x[1::2]
        n = 0
        for a in range(4):
            out[pl.ds(r, 16), n * 128:(n + 1) * 128] = (re[a] * re[a] + im[a] * im[a]).astype(bf16)
            n += 1
        for a in range(4):
            for b in range(a + 1, 4):
                x = re[a] * re[b] + im[a] * im[b]
                y = re[a] * im[b] - im[a] * re[b]
                if double:
                    x, y = x + x, y + y
                out[pl.ds(r, 16), n * 128:(n + 1) * 128] = x.astype(bf16)
                out[pl.ds(r, 16), (n + 1) * 128:(n + 2) * 128] = y.astype(bf16)
                n += 2

    def add_energy(i, energy):
        for step in range(STEPS):
            for q in range(4):
                r = step * SRC + q * 16
                x = [s_ref[q // 2, q % 2, i, step, n].astype(f32) for n in range(8)]
                for n in range(8):
                    s32[i, n, r:r + 16, :] = x[n]
                features(x, fs, False, r)
        for r in range(0, 2 * rows, 16):
            x = [w2[r:r + 16, pl.ds(pl.multiple_of(n * freq + i * 128, 128), 128)].astype(f32) for n in range(8)]
            features(x, fr, True, r)
        return energy + lax.dot_general(fs[...], fr[...], (((1,), (1,)), ((), ())),
                                        preferred_element_type=f32)

    energy = lax.fori_loop(0, freq // 128, add_energy, jnp.zeros((STEPS * SRC, 2 * rows), f32))
    scale = lax.rsqrt(jnp.maximum(energy, 0.0) * (1.0 / (2 * freq)) + pair_eps)

    rec = pos_ref[pl.ds(mine, 1), :].astype(f32)
    lane = lax.broadcasted_iota(jnp.int32, (SRC, 2 * rows), 1)
    rec_ids = mine * rows + lane % rows
    firsts = []
    for step in range(STEPS):
        block = order_ref[step]
        src = as_column(pos_ref[pl.ds(block, 1), :].astype(f32)[:, :SRC])
        pair_bins = to_bins(jnp.abs(src - rec), loop, bins)
        src_ids = block * SRC + lax.broadcasted_iota(jnp.int32, (SRC, 2 * rows), 0)
        weight = jnp.where(src_ids == rec_ids, 0.0, scale[step * SRC:(step + 1) * SRC])
        first = jnp.min(jnp.min(pair_bins, axis=1, keepdims=True), axis=0, keepdims=True)
        firsts.append(first)
        rel = pair_bins - first
        upper = rel >= float(SLOTS)
        slot = jnp.where(upper, rel - float(SLOTS), rel)
        for k in range(SLOTS):
            here = slot == float(k)
            part = jnp.where(here, weight, 0.0)
            high = part.astype(bf16)
            low = (part - high.astype(f32)).astype(bf16)
            amat[step, k * SRC:(k + 1) * SRC, :] = jnp.where(lane < rows, high.astype(f32), low.astype(f32)).astype(bf16)
            mark = jnp.max(jnp.where(here & upper, 1.0, 0.0), axis=1, keepdims=True)
            hmask[step, k * SRC:(k + 1) * SRC, :] = jnp.broadcast_to(mark, (SRC, 128))

    chunks = freq // 128
    total = STEPS * chunks

    def project(i, wf, t):
        step, col = i // chunks, (i % chunks) * 128
        for n in range(8):
            wf[:, n * 128:(n + 1) * 128] = w2[:, pl.ds(pl.multiple_of(n * freq + col, 128), 128)]
        t[...] = jnp.dot(amat[step], wf[...], preferred_element_type=f32)

    def gather(i, t):
        step, col = i // chunks, pl.multiple_of((i % chunks) * 128, 128)
        for k in range(SLOTS):
            sums = [None] * 4
            for g in range(SRC // 8):
                r = k * SRC + g * 8
                row = pl.multiple_of(step * SRC + g * 8, 8)
                re, im = [], []
                for a in range(4):
                    tr = t[r:r + 8, 2 * a * 128:(2 * a + 1) * 128]
                    ti = t[r:r + 8, (2 * a + 1) * 128:(2 * a + 2) * 128]
                    sr = s32[i % chunks, 2 * a, pl.ds(row, 8), :]
                    si = s32[i % chunks, 2 * a + 1, pl.ds(row, 8), :]
                    re += [sr * tr, si * ti]
                    im.append(sr * ti - si * tr)
                real = ((re[0] + re[1]) + (re[2] + re[3])) + ((re[4] + re[5]) + (re[6] + re[7]))
                imag = (im[0] + im[1]) + (im[2] + im[3])
                mark = hmask[step, r:r + 8, :]
                new = [real, imag, real * mark, imag * mark]
                sums = new if g == 0 else [x + y for x, y in zip(sums, new)]
            base = step * (2 * SLOTS * 8)
            acc[pl.ds(pl.multiple_of(base + k * 8, 8), 8), pl.ds(col, 128)] = sums[0]
            acc[pl.ds(pl.multiple_of(base + k * 8, 8), 8), pl.ds(pl.multiple_of(freq + col, 128), 128)] = sums[1]
            base = base + SLOTS * 8
            acc[pl.ds(pl.multiple_of(base + k * 8, 8), 8), pl.ds(col, 128)] = sums[2]
            acc[pl.ds(pl.multiple_of(base + k * 8, 8), 8), pl.ds(pl.multiple_of(freq + col, 128), 128)] = sums[3]

    project(0, wf0, t0)

    def pair(j, _):
        project(2 * j + 1, wf1, t1)
        gather(2 * j, t0)
        project(jnp.minimum(2 * j + 2, total - 1), wf0, t0)
        gather(2 * j + 1, t1)
        return 0

    lax.fori_loop(0, total // 2, pair, 0)

    span = 2 * SLOTS * 8
    col = lax.broadcasted_iota(jnp.int32, (bins, span), 1)
    row = lax.broadcasted_iota(jnp.int32, (bins, span), 0).astype(f32)
    marked = col >= SLOTS * 8
    k = ((col - jnp.where(marked, SLOTS * 8, 0)) // 8).astype(f32)
    place = []
    for step in range(STEPS):
        at = row == firsts[step] + k
        above = row == firsts[step] + k + float(SLOTS)
        place.append(jnp.where(marked, jnp.where(above, 1.0, 0.0) - jnp.where(at, 1.0, 0.0),
                               jnp.where(at, 1.0, 0.0)).astype(bf16))
    for c in range(0, width // 4, 256):
        out = jnp.zeros((bins, 256), f32)
        for step in range(STEPS):
            value = acc[step * span:(step + 1) * span, c:c + 256]
            high = value.astype(bf16)
            low = (value - high.astype(f32)).astype(bf16)
            out += jnp.dot(place[step], high, preferred_element_type=f32)
            out += jnp.dot(place[step], low, preferred_element_type=f32)
        out_ref[:, c:c + 256] = out


def correlate(white, sources, pos2, order, bins):
    rows, width = white.shape
    freq = width // 8
    vm = pl.BlockSpec(memory_space=pltpu.VMEM)
    return pl.pallas_call(
        functools.partial(corr_kernel, pos2.shape[0] * rows, bins),
        out_shape=jax.ShapeDtypeStruct((bins, 2 * freq), f32),
        in_specs=[pl.BlockSpec(memory_space=pltpu.SMEM), vm, vm, vm],
        out_specs=vm,
        scratch_shapes=[
            pltpu.VMEM((2 * rows, width), bf16),
            pltpu.VMEM((freq // 128, 8, STEPS * SRC, 128), f32),
            pltpu.VMEM((STEPS * SRC, 16 * 128), bf16),
            pltpu.VMEM((2 * rows, 16 * 128), bf16),
            pltpu.VMEM((STEPS, SLOTS * SRC, 2 * rows), bf16),
            pltpu.VMEM((STEPS, SLOTS * SRC, 128), f32),
            pltpu.VMEM((2 * rows, 1024), bf16),
            pltpu.VMEM((2 * rows, 1024), bf16),
            pltpu.VMEM((SLOTS * SRC, 1024), f32),
            pltpu.VMEM((SLOTS * SRC, 1024), f32),
            pltpu.VMEM((STEPS * 2 * SLOTS * 8, 2 * freq), f32),
        ],
        compiler_params=pltpu.CompilerParams(vmem_limit_bytes=56 * MIB),
        name="correlate",
    )(order, pos2, white, sources)


BIN_DEV = 4


def spread_kernel(n_chan, n_tm, order_ref, x_ref, w_ref, all_ref,
                  sib, part, got, inv, relay, relayed, keep, cross, crossed, ppart, pgot,
                  sib_sem, send1, recv1, send2, recv2, ring_send, ring_recv, cross_sem,
                  send3, recv3, swap_sem, out_send, out_recv, pass_send, pass_recv):
    rows, width = x_ref.shape
    freq = width // 8
    cols = freq // n_tm
    half, quarter = rows // 2, rows // 4
    me_c, me = lax.axis_index("chan"), lax.axis_index("tm")
    n_z = n_chan // 4
    z, hi, core = me_c // 4, lax.rem(me_c // 2, 2), lax.rem(me_c, 2)
    up, down = lax.rem(z + 1, n_z), lax.rem(z + n_z - 1, n_z)

    def chan(zz, hh, cc):
        return zz * 4 + hh * 2 + cc

    sibling, partner = chan(z, hi, 1 - core), chan(z, 1 - hi, core)
    ways = [chan(up, hi, core), chan(down, hi, core)]
    peers = [lax.rem(me + d, n_tm) for d in range(n_tm)]
    back = [lax.rem(me - d + n_tm, n_tm) for d in range(n_tm)]
    barrier = pltpu.get_barrier_semaphore()
    for d in range(1, n_tm):
        pl.semaphore_signal(barrier, inc=1, device_id={"chan": me_c, "tm": peers[d]})
    for other in [sibling, partner] + ways:
        pl.semaphore_signal(barrier, inc=1, device_id={"chan": other, "tm": me})
    pl.semaphore_wait(barrier, n_tm - 1 + 4)

    def remote(src, dst, send, recv, other_chan, other_tm):
        return pltpu.make_async_remote_copy(src_ref=src, dst_ref=dst, send_sem=send, recv_sem=recv,
                                            device_id={"chan": other_chan, "tm": other_tm})

    share = remote(x_ref.at[pl.ds(pl.multiple_of((1 - core) * half, half), half)], sib,
                   sib_sem.at[0], sib_sem.at[1], sibling, me)
    share.start()
    for p in range(n_tm):
        total = None
        for n in range(8):
            v = x_ref[:, n * freq + p * cols:n * freq + (p + 1) * cols].astype(f32)
            total = v * v if total is None else total + v * v
        part[p] = total.astype(bf16)
    first = [remote(part.at[peers[d]], got.at[me], send1.at[d], recv1.at[me], me_c, peers[d])
             for d in range(1, n_tm)]
    for copy in first:
        copy.start()
    share.wait()

    subs = ring_send.shape[2]
    per = 8 // subs
    blocks = [order_ref[k] for k in range(STEPS)]
    here = [blocks[k] // 4 == z for k in range(STEPS)]
    own_core = [lax.rem(blocks[k], 2) == core for k in range(STEPS)]
    mine_at = pl.ds(pl.multiple_of(core * half, half), half)

    def own(k, n, plane):
        at = pl.ds(pl.multiple_of(n * freq + plane * 128, 128), 128)
        return jnp.where(own_core[k], x_ref[mine_at, at], sib[:, at])

    def hop(k, t, s):
        n = pl.ds(s * per, per)
        return remote(relay.at[k, t, n], relayed.at[k, t, n], ring_send.at[k, t, s], ring_recv.at[k, t, s], ways[k], me)

    def ring_round(t, with_wait):
        for s in range(subs):
            for k in range(STEPS):
                plane = lax.rem(z + n_z - 1 - t, n_z) if k == 0 else lax.rem(z + t + 1, n_z)
                if with_wait:
                    hop(k, t - 1, s).wait_recv()
                for n in range(s * per, (s + 1) * per):
                    value = own(k, n, plane)
                    if with_wait:
                        value = jnp.where(here[k], value, relayed[k, t - 1, n])
                    relay[k, t, n] = value
                hop(k, t, s).start()

    ring_round(0, False)

    def more(t, _):
        ring_round(t, True)
        return 0

    middle = (n_z - 1) // 2 + 1
    lax.fori_loop(1, middle, more, 0)

    total = part[me].astype(f32)
    for d in range(1, n_tm):
        remote(part.at[me], got.at[back[d]], send1.at[d], recv1.at[back[d]], me_c, peers[d]).wait_recv()
        total = total + got[back[d]].astype(f32)
    inv[me] = 1.0 / jnp.sqrt(total * (1.0 / (4 * n_tm)) + water_level)
    second = [remote(inv.at[me], inv.at[me], send2.at[d], recv2.at[me], me_c, peers[d]) for d in range(1, n_tm)]
    for copy in second:
        copy.start()

    lax.fori_loop(middle, n_z - 1, more, 0)

    hi_at = pl.ds(pl.multiple_of(hi * quarter, quarter), quarter)
    low_at = pl.ds(pl.multiple_of((1 - hi) * quarter, quarter), quarter)
    for k in range(STEPS):
        for s in range(subs):
            hop(k, n_z - 2, s).wait_recv()
        for n in range(8):
            keep[k, n] = jnp.where(here[k], own(k, n, z), relayed[k, n_z - 2, n])
            cross[k, n] = keep[k, n, low_at, :]
    swap = remote(cross, crossed, cross_sem.at[0], cross_sem.at[1], partner, me)
    swap.start()
    swap.wait()
    raw = []
    for k in range(STEPS):
        from_here = lax.rem(blocks[k] // 2, 2) == hi
        total = None
        for n in range(8):
            v = jnp.where(from_here, keep[k, n, hi_at, :], crossed[k, n])
            keep[k, n, :quarter] = v
            v = v.astype(f32)
            total = v * v if total is None else total + v * v
        ppart[k * quarter:(k + 1) * quarter] = total.astype(bf16)
    third = [remote(ppart, pgot.at[me], send3.at[d], recv3.at[me], me_c, peers[d]) for d in range(1, n_tm)]
    for copy in third:
        copy.start()

    def whiten(p):
        factor = inv[p]
        for n in range(8):
            at = pl.ds(pl.multiple_of(n * freq + p * cols, cols), cols)
            w_ref[:, at] = (x_ref[:, at].astype(f32) * factor).astype(bf16)

    whiten(me)
    for d in range(1, n_tm):
        remote(inv.at[me], inv.at[back[d]], send2.at[d], recv2.at[back[d]], me_c, peers[d]).wait_recv()
        whiten(back[d])

    total = ppart[...].astype(f32)
    for d in range(1, n_tm):
        remote(ppart, pgot.at[back[d]], send3.at[d], recv3.at[back[d]], me_c, peers[d]).wait_recv()
        total = total + pgot[back[d]].astype(f32)
    factor = 1.0 / jnp.sqrt(total * (1.0 / (4 * n_tm)) + water_level)
    for k in range(STEPS):
        for n in range(8):
            all_ref[core, hi, z, k, n] = (keep[k, n, :quarter].astype(f32)
                                          * factor[k * quarter:(k + 1) * quarter]).astype(bf16)

    side = remote(all_ref.at[core, hi, z], all_ref.at[core, hi, z], swap_sem.at[0], swap_sem.at[1], partner, me)
    side.start()
    side.wait()

    def send_on(w, t, s):
        plane = lax.rem(z + n_z - t, n_z) if w == 0 else lax.rem(z + t, n_z)
        ref = all_ref.at[core, w, plane, s // 2, pl.ds((s % 2) * 4, 4)]
        return remote(ref, ref, out_send.at[w, t, s], out_recv.at[w, t, s], ways[w], me)

    def came(w, t, s):
        plane = lax.rem(z + n_z - t - 1, n_z) if w == 0 else lax.rem(z + t + 1, n_z)
        ref = all_ref.at[core, w, plane, s // 2, pl.ds((s % 2) * 4, 4)]
        return remote(ref, ref, out_send.at[w, t, s], out_recv.at[w, t, s], ways[w], me)

    def pass_over(w, t):
        plane = lax.rem(z + n_z - t, n_z) if w == 0 else lax.rem(z + t, n_z)
        ref = all_ref.at[core, w, plane]
        return remote(ref, ref, pass_send.at[w, t], pass_recv.at[w, t], sibling, me)

    def passed(w, t):
        plane = lax.rem(z + n_z - t, n_z) if w == 0 else lax.rem(z + t, n_z)
        ref = all_ref.at[1 - core, w, plane]
        return remote(ref, ref, pass_send.at[w, t], pass_recv.at[w, t], sibling, me)

    for w in range(2):
        for s in range(4):
            send_on(w, 0, s).start()
        pass_over(w, 0).start()

    def onward(t, _):
        for s in range(4):
            for w in range(2):
                came(w, t - 1, s).wait_recv()
                send_on(w, t, s).start()
        for w in range(2):
            pass_over(w, t).start()
        return 0

    lax.fori_loop(1, n_z - 1, onward, 0)
    for w in range(2):
        for s in range(4):
            came(w, n_z - 2, s).wait_recv()
        pass_over(w, n_z - 1).start()

    def finish(t, _):
        for w in range(2):
            passed(w, t).wait_recv()
            pass_over(w, t).wait_send()
        return 0

    lax.fori_loop(0, n_z, finish, 0)

    def sent(t, _):
        for w in range(2):
            for s in range(4):
                send_on(w, t, s).wait_send()
            for s in range(subs):
                hop(w, t, s).wait_send()
        return 0

    lax.fori_loop(0, n_z - 1, sent, 0)
    for copy in first + second + third:
        copy.wait_send()


def spread(flat, order, n_chan, n_tm):
    rows, width = flat.shape
    cols = width // 8 // n_tm
    n_z = n_chan // 4
    subs = 4
    half, quarter = rows // 2, rows // 4
    vm = pl.BlockSpec(memory_space=pltpu.VMEM)
    dma = pltpu.SemaphoreType.DMA
    return pl.pallas_call(
        functools.partial(spread_kernel, n_chan, n_tm),
        out_shape=[jax.ShapeDtypeStruct((rows, width), bf16),
                   jax.ShapeDtypeStruct((2, 2, n_z, STEPS, 8, quarter, 128), bf16)],
        in_specs=[pl.BlockSpec(memory_space=pltpu.SMEM), vm],
        out_specs=[vm, vm],
        scratch_shapes=[
            pltpu.VMEM((half, width), bf16),
            pltpu.VMEM((n_tm, rows, cols), bf16),
            pltpu.VMEM((n_tm, rows, cols), bf16),
            pltpu.VMEM((n_tm, rows, cols), f32),
            pltpu.VMEM((STEPS, n_z - 1, 8, half, 128), bf16),
            pltpu.VMEM((STEPS, n_z - 1, 8, half, 128), bf16),
            pltpu.VMEM((STEPS, 8, half, 128), bf16),
            pltpu.VMEM((STEPS, 8, quarter, 128), bf16),
            pltpu.VMEM((STEPS, 8, quarter, 128), bf16),
            pltpu.VMEM((STEPS * quarter, 128), bf16),
            pltpu.VMEM((n_tm, STEPS * quarter, 128), bf16),
            dma((2,)), dma((n_tm,)), dma((n_tm,)), dma((n_tm,)), dma((n_tm,)),
            dma((STEPS, n_z - 1, subs)), dma((STEPS, n_z - 1, subs)), dma((2,)),
            dma((n_tm,)), dma((n_tm,)), dma((2,)),
            dma((2, n_z - 1, 4)), dma((2, n_z - 1, 4)), dma((2, n_z)), dma((2, n_z)),
        ],
        compiler_params=pltpu.CompilerParams(collective_id=0, has_side_effects=True, vmem_limit_bytes=48 * MIB),
        name="spread",
    )(order, flat)


def reduce_kernel(n_chan, n_tm, channels, bins, order_ref, pos_ref, stack_ref, table_ref, out_ref,
                  table, out0, got0, out1, got1, out2, got2, parts, xk,
                  table_sem, sem0, send1, recv1, send2, recv2, send3, recv3):
    width = stack_ref.shape[1]
    freq = width // 2
    loop = float(channels + 1 + (channels - 1) // 2)
    me_c, me_t = lax.axis_index("chan"), lax.axis_index("tm")
    zh, core = me_c // 2, lax.rem(me_c, 2)
    n_zh = n_chan // 2
    cols = freq // n_tm
    sibling = zh * 2 + 1 - core
    tms = [lax.rem(me_t + d, n_tm) for d in range(n_tm)]
    zhs = [lax.rem(zh + d, n_zh) for d in range(n_zh)]
    group = [(me_c, core, tms[d]) for d in range(1, n_tm)] + [(sibling, 1 - core, tms[d]) for d in range(n_tm)]
    back = [lax.rem(me_t - d + n_tm, n_tm) for d in range(n_tm)]
    group_back = [(core, back[d]) for d in range(1, n_tm)] + [(1 - core, back[d]) for d in range(n_tm)]
    barrier = pltpu.get_barrier_semaphore()
    for chan, _, tm in group:
        pl.semaphore_signal(barrier, inc=1, device_id={"chan": chan, "tm": tm})
    for q in zhs[1:]:
        pl.semaphore_signal(barrier, inc=1, device_id={"chan": q * 2 + core, "tm": me_t})
    load = pltpu.make_async_copy(table_ref, table, table_sem.at[0])
    load.start()

    def remote(src, dst, send, recv, chan, tm):
        return pltpu.make_async_remote_copy(src_ref=src, dst_ref=dst, send_sem=send, recv_sem=recv,
                                            device_id={"chan": chan, "tm": tm})

    out0[...] = stack_ref[:, pl.ds(pl.multiple_of((1 - core) * freq, freq), freq)].astype(bf16)
    pl.semaphore_wait(barrier, len(group) + n_zh - 1)
    swap = remote(out0, got0, sem0.at[0], sem0.at[1], sibling, me_t)
    swap.start()

    counts = []
    for step in range(STEPS):
        src = as_column(pos_ref[pl.ds(order_ref[step], 1), :].astype(f32)[:, :SRC])

        def count(i, sums):
            pair_bins = to_bins(jnp.abs(src - pos_ref[pl.ds(i, 1), :].astype(f32)), loop, bins)
            rel = pair_bins - (me_c * BIN_DEV).astype(f32)
            return tuple(s + jnp.where(rel == float(b), 0.5, 0.0) for b, s in enumerate(sums))

        init = tuple(jnp.zeros((SRC, pos_ref.shape[1]), f32) for _ in range(BIN_DEV))
        counts.append(lax.fori_loop(0, pos_ref.shape[0], count, init))
    factors = []
    for b in range(BIN_DEV):
        amount = sum(c[b] for c in counts)
        amount = jnp.sum(jnp.sum(amount, axis=1, keepdims=True), axis=0, keepdims=True)
        own = jnp.where(me_c * BIN_DEV + b == 0, float(STEPS * SRC), 0.0)
        factors.append(lax.rsqrt((amount - own) * float(n_tm * freq)))
    factor = jnp.concatenate(factors, 0)

    swap.wait()
    for p in range(n_tm):
        at = pl.ds(pl.multiple_of(core * freq + p * cols, cols), cols)
        out1[p] = (stack_ref[:, at] + got0[:, p * cols:(p + 1) * cols].astype(f32)).astype(bf16)
    first = [remote(out1.at[tms[d]], got1.at[me_t], send1.at[d], recv1.at[me_t], me_c, tms[d])
             for d in range(1, n_tm)]
    for copy in first:
        copy.start()
    total = out1[me_t].astype(f32)
    for d in range(1, n_tm):
        remote(out1.at[me_t], got1.at[back[d]], send1.at[d], recv1.at[back[d]], me_c, tms[d]).wait_recv()
        total = total + got1[back[d]].astype(f32)
    out2[...] = total.reshape(out2.shape)
    second = [remote(out2.at[zhs[d]], got2.at[zh], send2.at[d], recv2.at[zh], zhs[d] * 2 + core, me_t)
              for d in range(1, n_zh)]
    for copy in second:
        copy.start()
    total = out2[zh]
    for d in range(1, n_zh):
        other = lax.rem(zh - d + n_zh, n_zh)
        remote(out2.at[zh], got2.at[other], send2.at[d], recv2.at[other], zhs[d] * 2 + core, me_t).wait_recv()
        total = total + got2[other]
    slot = core * n_tm + me_t
    parts[slot] = total
    third = [remote(parts.at[slot], parts.at[slot], send3.at[i], recv3.at[slot], chan, tm)
             for i, (chan, _, tm) in enumerate(group)]
    for copy in third:
        copy.start()
    for i, ((chan, _, tm), (c, t)) in enumerate(zip(group, group_back)):
        other = c * n_tm + t
        remote(parts.at[slot], parts.at[other], send3.at[i], recv3.at[other], chan, tm).wait_recv()
    for n in range(2 * n_tm):
        value = parts[n]
        high = value.astype(bf16).astype(f32)
        xk[:, n * cols:(n + 1) * cols] = jnp.concatenate([high, value - high], 0).astype(bf16)
    load.wait()
    piece = 512
    for c in range(0, width, piece):
        both = jnp.dot(xk[...], table[:, c:c + piece], preferred_element_type=f32)
        both = both[:8] + both[8:]
        out_ref[:, c:c + piece] = jnp.where(core == 0, both[:BIN_DEV], both[BIN_DEV:]) * factor
    for copy in first + second + third:
        copy.wait_send()


def lag_table(freq):
    width = 2 * freq
    phase = np.outer(np.arange(freq), np.arange(width) - freq) % width
    angle = 2.0 * np.pi / width * phase
    return np.concatenate([np.cos(angle), -np.sin(angle)], 0).astype(jnp.bfloat16)


def reduce_stack(stack, pos2, order, n_chan, n_tm, channels):
    bins, width = stack.shape
    cols = width // 2 // n_tm
    n_zh = n_chan // 2
    vm = pl.BlockSpec(memory_space=pltpu.VMEM)
    dma = pltpu.SemaphoreType.DMA
    return pl.pallas_call(
        functools.partial(reduce_kernel, n_chan, n_tm, channels, bins),
        out_shape=jax.ShapeDtypeStruct((BIN_DEV, width), f32),
        in_specs=[pl.BlockSpec(memory_space=pltpu.SMEM), vm, vm, pl.BlockSpec(memory_space=pl.ANY)],
        out_specs=vm,
        scratch_shapes=[
            pltpu.VMEM((width, width), bf16),
            pltpu.VMEM((bins, width // 2), bf16),
            pltpu.VMEM((bins, width // 2), bf16),
            pltpu.VMEM((n_tm, bins, cols), bf16),
            pltpu.VMEM((n_tm, bins, cols), bf16),
            pltpu.VMEM((n_zh, bins // n_zh, cols), f32),
            pltpu.VMEM((n_zh, bins // n_zh, cols), f32),
            pltpu.VMEM((2 * n_tm, bins // n_zh, cols), f32),
            pltpu.VMEM((16, width), bf16),
            dma((1,)), dma((2,)), dma((n_tm,)), dma((n_tm,)), dma((n_zh,)), dma((n_zh,)),
            dma((2 * n_tm,)), dma((2 * n_tm,)),
        ],
        compiler_params=pltpu.CompilerParams(collective_id=1, has_side_effects=True, vmem_limit_bytes=48 * MIB),
        name="reduce_stack",
    )(order, pos2, stack, jnp.asarray(lag_table(width // 2)))


def local(spectra, positions, source_order):
    rows, seg_dev, width = spectra.shape
    n_chan = lax.axis_size("chan")
    n_tm = lax.axis_size("tm")
    bins = BIN_DEV * n_chan
    channels = n_chan * rows
    flat = spectra.reshape(rows, seg_dev * width)
    white, sources = spread(flat, source_order, n_chan, n_tm)
    pos2 = positions.reshape(n_chan, rows)
    pos2 = jnp.concatenate([pos2, pos2], 1)
    stack = correlate(white, sources, pos2, source_order, bins)
    return reduce_stack(stack, pos2, source_order, n_chan, n_tm, channels)


def solution(mesh):
    return jax.shard_map(
        local,
        mesh=mesh,
        in_specs=(P("chan", "tm", None), P(), P()),
        out_specs=P("chan", None),
        check_vma=False,
    )
```

```python
import functools

import jax
import jax.numpy as jnp
import numpy as np
from jax import lax
from jax.experimental import pallas as pl
from jax.experimental.pallas import tpu as pltpu
from jax.sharding import PartitionSpec as P

SRC = 64
STEPS = 2
SLOTS = 12
BIN_DEV = 4
MIB = 1024 * 1024

water_level = 0.1
pair_eps = 1e-06
f32 = jnp.float32
bf16 = jnp.bfloat16


def to_bins(gap, loop, bins):
    offset = jnp.minimum(gap, loop - gap)
    return jnp.floor((offset * (2 * bins) + 0.5) * (1.0 / (loop + 1)))


def as_column(row):
    n = row.shape[1]
    eye = lax.broadcasted_iota(jnp.int32, (n, n), 0) == lax.broadcasted_iota(jnp.int32, (n, n), 1)
    return jnp.sum(jnp.where(eye, row, 0.0), axis=1, keepdims=True)


def features(x, out, double):
    re, im = x[0::2], x[1::2]
    n = 0
    for a in range(4):
        out(n, re[a] * re[a] + im[a] * im[a])
        n += 1
    for a in range(4):
        for b in range(a + 1, 4):
            real = re[a] * re[b] + im[a] * im[b]
            imag = re[a] * im[b] - im[a] * re[b]
            if double:
                real, imag = real + real, imag + imag
            out(n, real)
            out(n + 1, imag)
            n += 2


def kernel(n_chan, n_tm, order_ref, pos_ref, x_ref, table_ref, out_ref,
           sib, part, got, inv, relay, relayed, keep, crossed, ppart, pgot, pieces,
           w2, s32, fs, fr, amat, hmask, wf0, wf1, t0, t1, acc,
           stack, table, out0, got0, out1, got1, out2, got2, owned, xk,
           table_sem, share_sem, send1, recv1, send2, recv2, ring_send, ring_recv, cross_sem,
           send3, recv3, around_send, around_recv, pass_send, pass_recv,
           swap_sem, send4, recv4, send5, recv5, send6, recv6):
    rows, width = x_ref.shape
    freq = width // 8
    cols = freq // n_tm
    half = rows // 2
    bins = BIN_DEV * n_chan
    channels = n_chan * rows
    loop = float(channels + 1 + (channels - 1) // 2)
    me_c, me = lax.axis_index("chan"), lax.axis_index("tm")
    n_z, n_zh = n_chan // 4, n_chan // 2
    zh, core = me_c // 2, lax.rem(me_c, 2)
    z, hi = zh // 2, lax.rem(zh, 2)
    sibling, partner = zh * 2 + 1 - core, z * 4 + (1 - hi) * 2 + core

    def above(d):
        return lax.rem(z + d + n_z, n_z)

    ways = [above(1) * 4 + hi * 2 + core, above(-1) * 4 + hi * 2 + core]
    reach = [n_z // 2, n_z - 1 - n_z // 2]
    tms = [lax.rem(me + d, n_tm) for d in range(n_tm)]
    back = [lax.rem(me - d + n_tm, n_tm) for d in range(n_tm)]
    zhs = [lax.rem(zh + d, n_zh) for d in range(n_zh)]
    group = [(me_c, core, tms[d]) for d in range(1, n_tm)] + [(sibling, 1 - core, tms[d]) for d in range(n_tm)]
    group_back = [(core, back[d]) for d in range(1, n_tm)] + [(1 - core, back[d]) for d in range(n_tm)]

    barrier = pltpu.get_barrier_semaphore()
    for chan, _, tm in group:
        pl.semaphore_signal(barrier, inc=1, device_id={"chan": chan, "tm": tm})
    for q in zhs[1:]:
        pl.semaphore_signal(barrier, inc=1, device_id={"chan": q * 2 + core, "tm": me})
    load = pltpu.make_async_copy(table_ref, table, table_sem.at[0])
    load.start()

    def remote(src, dst, send, recv, chan, tm):
        return pltpu.make_async_remote_copy(src_ref=src, dst_ref=dst, send_sem=send, recv_sem=recv,
                                            device_id={"chan": chan, "tm": tm})

    for p in range(n_tm):
        total = None
        for n in range(8):
            v = x_ref[:, n * freq + p * cols:n * freq + (p + 1) * cols].astype(f32)
            total = v * v if total is None else total + v * v
        part[p] = total.astype(bf16)
    pl.semaphore_wait(barrier, len(group) + n_zh - 1)

    share = remote(x_ref.at[pl.ds(pl.multiple_of((1 - core) * half, half), half)], sib,
                   share_sem.at[0], share_sem.at[1], sibling, me)
    share.start()
    first = [remote(part.at[tms[d]], got.at[me], send1.at[d], recv1.at[me], me_c, tms[d]) for d in range(1, n_tm)]
    for copy in first:
        copy.start()
    share.wait()

    blocks = [order_ref[k] for k in range(STEPS)]
    ahead = [lax.rem(z - blocks[k] // 4 + n_z, n_z) for k in range(STEPS)]
    own_core = [lax.rem(blocks[k], 2) == core for k in range(STEPS)]
    mine_at = pl.ds(pl.multiple_of(core * half, half), half)
    subs = [(k, s) for k in range(STEPS) for s in range(2)]

    def own(k, n, plane):
        at = pl.ds(pl.multiple_of(n * freq + plane * 128, 128), 128)
        return jnp.where(own_core[k], x_ref[mine_at, at], sib[:, at])

    def hop(w, t, k, s):
        n = pl.ds(s * 4, 4)
        return remote(relay.at[w, t, k, n], relayed.at[w, t, k, n], ring_send.at[w, t, 2 * k + s],
                      ring_recv.at[w, t, 2 * k + s], ways[w], me)

    def ring_round(t):
        for k, s in subs:
            for w in range(2):
                if t >= reach[w]:
                    continue
                plane = above(reach[w] - t) if w == 0 else above(t - reach[w])
                if t:
                    hop(w, t - 1, k, s).wait_recv()
                for n in range(s * 4, s * 4 + 4):
                    value = own(k, n, plane)
                    if t:
                        value = jnp.where(ahead[k] == 0, value, relayed[w, t - 1, k, n])
                    relay[w, t, k, n] = value
                hop(w, t, k, s).start()

    ring_round(0)

    counts = []
    for k in range(STEPS):
        src = as_column(pos_ref[pl.ds(blocks[k], 1), :].astype(f32)[:, :SRC])

        def count(i, sums):
            pair_bins = to_bins(jnp.abs(src - pos_ref[pl.ds(i, 1), :].astype(f32)), loop, bins)
            rel = pair_bins - (me_c * BIN_DEV).astype(f32)
            return tuple(s + jnp.where(rel == float(b), 0.5, 0.0) for b, s in enumerate(sums))

        init = tuple(jnp.zeros((SRC, pos_ref.shape[1]), f32) for _ in range(BIN_DEV))
        counts.append(lax.fori_loop(0, pos_ref.shape[0], count, init))
    factors = []
    for b in range(BIN_DEV):
        amount = sum(c[b] for c in counts)
        amount = jnp.sum(jnp.sum(amount, axis=1, keepdims=True), axis=0, keepdims=True)
        alone = jnp.where(me_c * BIN_DEV + b == 0, float(STEPS * SRC), 0.0)
        factors.append(lax.rsqrt((amount - alone) * float(n_tm * freq)))
    norm = jnp.concatenate(factors, 0)

    ring_round(1)

    total = part[me].astype(f32)
    for d in range(1, n_tm):
        remote(part.at[me], got.at[back[d]], send1.at[d], recv1.at[back[d]], me_c, tms[d]).wait_recv()
        total = total + got[back[d]].astype(f32)
    inv[me] = 1.0 / jnp.sqrt(total * (1.0 / (4 * n_tm)) + water_level)
    second = [remote(inv.at[me], inv.at[me], send2.at[d], recv2.at[me], me_c, tms[d]) for d in range(1, n_tm)]
    for copy in second:
        copy.start()

    for t in range(2, reach[0]):
        ring_round(t)

    for k, s in subs:
        for w in range(2):
            hop(w, reach[w] - 1, k, s).wait_recv()
        for n in range(s * 4, s * 4 + 4):
            value = jnp.where(ahead[k] <= reach[0], relayed[0, reach[0] - 1, k, n], relayed[1, reach[1] - 1, k, n])
            keep[k, n] = jnp.where(ahead[k] == 0, own(k, n, z), value)
    cross = remote(keep, crossed, cross_sem.at[0], cross_sem.at[1], partner, me)
    cross.start()

    def whiten(p):
        factor = inv[p]
        for n in range(8):
            at = pl.ds(pl.multiple_of(n * freq + p * cols, cols), cols)
            value = (x_ref[:, at].astype(f32) * factor).astype(bf16)
            w2[:rows, at] = value
            w2[rows:, at] = value

    whiten(me)
    for d in range(1, n_tm):
        remote(inv.at[me], inv.at[back[d]], send2.at[d], recv2.at[back[d]], me_c, tms[d]).wait_recv()
        whiten(back[d])

    cross.wait()
    for k in range(STEPS):
        from_here = lax.rem(blocks[k] // 2, 2) == hi
        total = None
        for n in range(8):
            value = jnp.where(from_here, keep[k, n], crossed[k, n])
            keep[k, n] = value
            value = value.astype(f32)
            total = value * value if total is None else total + value * value
        ppart[k * half:(k + 1) * half] = total.astype(bf16)
    third = [remote(ppart, pgot.at[me], send3.at[d], recv3.at[me], me_c, tms[d]) for d in range(1, n_tm)]
    for copy in third:
        copy.start()

    def receiver_features(i, _):
        for r in range(0, rows, 16):
            x = [w2[r:r + 16, pl.ds(pl.multiple_of(n * freq + i * 128, 128), 128)].astype(f32) for n in range(8)]

            def out(n, value):
                value = value.astype(bf16)
                fr[i, r:r + 16, n * 128:(n + 1) * 128] = value
                fr[i, rows + r:rows + r + 16, n * 128:(n + 1) * 128] = value

            features(x, out, True)
        return 0

    lax.fori_loop(0, n_z, receiver_features, 0)

    total = ppart[...].astype(f32)
    for d in range(1, n_tm):
        remote(ppart, pgot.at[back[d]], send3.at[d], recv3.at[back[d]], me_c, tms[d]).wait_recv()
        total = total + pgot[back[d]].astype(f32)
    factor = 1.0 / jnp.sqrt(total * (1.0 / (4 * n_tm)) + water_level)
    for k in range(STEPS):
        for n in range(8):
            pieces[core, z, k, n] = (keep[k, n].astype(f32) * factor[k * half:(k + 1) * half]).astype(bf16)

    def around(w, t, k, s, arriving):
        d = t + 1 if arriving else t
        ref = pieces.at[core, above(-d) if w == 0 else above(d), k, pl.ds(s * 4, 4)]
        return remote(ref, ref, around_send.at[w, t, 2 * k + s], around_recv.at[w, t, 2 * k + s], ways[w], me)

    def pass_over(d, c):
        ref = pieces.at[c, above(d)]
        slot = d + n_z // 2
        return remote(ref, ref, pass_send.at[slot], pass_recv.at[slot], sibling, me)

    def add_energy(d, energy):
        pass_over(d, 1 - core).wait_recv()
        plane = above(d)
        for k in range(STEPS):
            for q in range(4):
                r = k * SRC + q * 16
                x = [pieces[q // 2, plane, k, n, (q % 2) * 16:(q % 2) * 16 + 16, :].astype(f32) for n in range(8)]
                for n in range(8):
                    s32[plane, n, r:r + 16, :] = x[n]

                def out(n, value):
                    fs[r:r + 16, n * 128:(n + 1) * 128] = value.astype(bf16)

                features(x, out, False)
        return energy + lax.dot_general(fs[...], fr[plane], (((1,), (1,)), ((), ())), preferred_element_type=f32)

    for k, s in subs:
        for w in range(2):
            around(w, 0, k, s, False).start()
    pass_over(0, core).start()
    energy = jnp.zeros((STEPS * SRC, 2 * rows), f32)
    for t in range(1, reach[0] + 1):
        for k, s in subs:
            for w in range(2):
                if t <= reach[w]:
                    around(w, t - 1, k, s, True).wait_recv()
                if t < reach[w]:
                    around(w, t, k, s, False).start()
        pass_over(-t, core).start()
        if t <= reach[1]:
            pass_over(t, core).start()
        energy = add_energy(1 - t, energy)
        if t > 1 and t - 1 <= reach[1]:
            energy = add_energy(t - 1, energy)
    energy = add_energy(-reach[0], energy)
    scale = lax.rsqrt(jnp.maximum(energy, 0.0) * (1.0 / (2 * freq)) + pair_eps)

    rec = pos_ref[pl.ds(me_c, 1), :].astype(f32)
    lane = lax.broadcasted_iota(jnp.int32, (SRC, 2 * rows), 1)
    rec_ids = me_c * rows + lane % rows
    firsts = []
    for step in range(STEPS):
        block = blocks[step]
        src = as_column(pos_ref[pl.ds(block, 1), :].astype(f32)[:, :SRC])
        pair_bins = to_bins(jnp.abs(src - rec), loop, bins)
        src_ids = block * SRC + lax.broadcasted_iota(jnp.int32, (SRC, 2 * rows), 0)
        weight = jnp.where(src_ids == rec_ids, 0.0, scale[step * SRC:(step + 1) * SRC])
        lowest = jnp.min(jnp.min(pair_bins, axis=1, keepdims=True), axis=0, keepdims=True)
        firsts.append(lowest)
        rel = pair_bins - lowest
        upper = rel >= float(SLOTS)
        slot = jnp.where(upper, rel - float(SLOTS), rel)
        for k in range(SLOTS):
            here = slot == float(k)
            value = jnp.where(here, weight, 0.0)
            high = value.astype(bf16).astype(f32)
            amat[step, k * SRC:(k + 1) * SRC, :] = jnp.where(lane < rows, high, value - high).astype(bf16)
            mark = jnp.max(jnp.where(here & upper, 1.0, 0.0), axis=1, keepdims=True)
            hmask[step, k * SRC:(k + 1) * SRC, :] = jnp.broadcast_to(mark, (SRC, 128))

    chunks = freq // 128
    amount = STEPS * chunks

    def project(i, wf, t):
        step, col = i // chunks, (i % chunks) * 128
        for n in range(8):
            wf[:, n * 128:(n + 1) * 128] = w2[:, pl.ds(pl.multiple_of(n * freq + col, 128), 128)]
        t[...] = jnp.dot(amat[step], wf[...], preferred_element_type=f32)

    def gather(i, t):
        step, chunk = i // chunks, i % chunks
        col = pl.multiple_of(chunk * 128, 128)
        for k in range(SLOTS):
            sums = [None] * 4
            for g in range(SRC // 8):
                r = k * SRC + g * 8
                row = pl.multiple_of(step * SRC + g * 8, 8)
                re, im = [], []
                for a in range(4):
                    tr = t[r:r + 8, 2 * a * 128:(2 * a + 1) * 128]
                    ti = t[r:r + 8, (2 * a + 1) * 128:(2 * a + 2) * 128]
                    sr = s32[chunk, 2 * a, pl.ds(row, 8), :]
                    si = s32[chunk, 2 * a + 1, pl.ds(row, 8), :]
                    re += [sr * tr, si * ti]
                    im.append(sr * ti - si * tr)
                real = ((re[0] + re[1]) + (re[2] + re[3])) + ((re[4] + re[5]) + (re[6] + re[7]))
                imag = (im[0] + im[1]) + (im[2] + im[3])
                mark = hmask[step, r:r + 8, :]
                new = [real, imag, real * mark, imag * mark]
                sums = new if g == 0 else [x + y for x, y in zip(sums, new)]
            for part_n in range(2):
                base = pl.multiple_of(step * (2 * SLOTS * 8) + part_n * (SLOTS * 8) + k * 8, 8)
                acc[pl.ds(base, 8), pl.ds(col, 128)] = sums[2 * part_n]
                acc[pl.ds(base, 8), pl.ds(pl.multiple_of(freq + col, 128), 128)] = sums[2 * part_n + 1]

    project(0, wf0, t0)

    def pair(j, _):
        project(2 * j + 1, wf1, t1)
        gather(2 * j, t0)
        project(jnp.minimum(2 * j + 2, amount - 1), wf0, t0)
        gather(2 * j + 1, t1)
        return 0

    lax.fori_loop(0, amount // 2, pair, 0)

    span = 2 * SLOTS * 8
    col = lax.broadcasted_iota(jnp.int32, (bins, span), 1)
    row = lax.broadcasted_iota(jnp.int32, (bins, span), 0).astype(f32)
    marked = col >= SLOTS * 8
    k = ((col - jnp.where(marked, SLOTS * 8, 0)) // 8).astype(f32)
    place = []
    for step in range(STEPS):
        at = row == firsts[step] + k
        higher = row == firsts[step] + k + float(SLOTS)
        place.append(jnp.where(marked, jnp.where(higher, 1.0, 0.0) - jnp.where(at, 1.0, 0.0),
                               jnp.where(at, 1.0, 0.0)).astype(bf16))
    for c in range(0, 2 * freq, 256):
        out = jnp.zeros((bins, 256), f32)
        for step in range(STEPS):
            value = acc[step * span:(step + 1) * span, c:c + 256]
            high = value.astype(bf16)
            low = (value - high.astype(f32)).astype(bf16)
            out += jnp.dot(place[step], high, preferred_element_type=f32)
            out += jnp.dot(place[step], low, preferred_element_type=f32)
        stack[:, c:c + 256] = out

    out0[...] = stack[:, pl.ds(pl.multiple_of((1 - core) * freq, freq), freq)].astype(bf16)
    swap = remote(out0, got0, swap_sem.at[0], swap_sem.at[1], sibling, me)
    swap.start()
    swap.wait()
    for p in range(n_tm):
        at = pl.ds(pl.multiple_of(core * freq + p * cols, cols), cols)
        out1[p] = (stack[:, at] + got0[:, p * cols:(p + 1) * cols].astype(f32)).astype(bf16)
    fourth = [remote(out1.at[tms[d]], got1.at[me], send4.at[d], recv4.at[me], me_c, tms[d]) for d in range(1, n_tm)]
    for copy in fourth:
        copy.start()
    total = out1[me].astype(f32)
    for d in range(1, n_tm):
        remote(out1.at[me], got1.at[back[d]], send4.at[d], recv4.at[back[d]], me_c, tms[d]).wait_recv()
        total = total + got1[back[d]].astype(f32)
    out2[...] = total.reshape(out2.shape)
    fifth = [remote(out2.at[zhs[d]], got2.at[zh], send5.at[d], recv5.at[zh], zhs[d] * 2 + core, me)
             for d in range(1, n_zh)]
    for copy in fifth:
        copy.start()
    total = out2[zh]
    for d in range(1, n_zh):
        other = lax.rem(zh - d + n_zh, n_zh)
        remote(out2.at[zh], got2.at[other], send5.at[d], recv5.at[other], zhs[d] * 2 + core, me).wait_recv()
        total = total + got2[other]
    slot = core * n_tm + me
    owned[slot] = total
    sixth = [remote(owned.at[slot], owned.at[slot], send6.at[i], recv6.at[slot], chan, tm)
             for i, (chan, _, tm) in enumerate(group)]
    for copy in sixth:
        copy.start()
    for i, ((chan, _, tm), (c, t)) in enumerate(zip(group, group_back)):
        other = c * n_tm + t
        remote(owned.at[slot], owned.at[other], send6.at[i], recv6.at[other], chan, tm).wait_recv()
    for n in range(2 * n_tm):
        value = owned[n]
        high = value.astype(bf16).astype(f32)
        xk[:, n * cols:(n + 1) * cols] = jnp.concatenate([high, value - high], 0).astype(bf16)
    load.wait()
    piece = 512
    for c in range(0, 2 * freq, piece):
        both = jnp.dot(xk[...], table[:, c:c + piece], preferred_element_type=f32)
        both = both[:8] + both[8:]
        out_ref[:, c:c + piece] = jnp.where(core == 0, both[:BIN_DEV], both[BIN_DEV:]) * norm

    for w in range(2):
        for t in range(reach[w]):
            for k, s in subs:
                hop(w, t, k, s).wait_send()
                around(w, t, k, s, False).wait_send()
    for d in range(-reach[0], reach[1] + 1):
        pass_over(d, core).wait_send()
    for copy in first + second + third + fourth + fifth + sixth:
        copy.wait_send()


def lag_table(freq):
    width = 2 * freq
    phase = np.outer(np.arange(freq), np.arange(width) - freq) % width
    angle = 2.0 * np.pi / width * phase
    return np.concatenate([np.cos(angle), -np.sin(angle)], 0).astype(jnp.bfloat16)


def local(spectra, positions, source_order):
    rows, seg_dev, lags = spectra.shape
    n_chan = lax.axis_size("chan")
    n_tm = lax.axis_size("tm")
    bins = BIN_DEV * n_chan
    flat = spectra.reshape(rows, seg_dev * lags)
    pos2 = positions.reshape(n_chan, rows)
    pos2 = jnp.concatenate([pos2, pos2], 1)
    width = seg_dev * lags
    freq = lags // 2
    cols = freq // n_tm
    n_z, n_zh = n_chan // 4, n_chan // 2
    half = rows // 2
    up = n_z // 2
    vm = pl.BlockSpec(memory_space=pltpu.VMEM)
    dma = pltpu.SemaphoreType.DMA
    vmem = pltpu.VMEM
    return pl.pallas_call(
        functools.partial(kernel, n_chan, n_tm),
        out_shape=jax.ShapeDtypeStruct((BIN_DEV, lags), f32),
        in_specs=[pl.BlockSpec(memory_space=pltpu.SMEM), vm, vm, pl.BlockSpec(memory_space=pl.ANY)],
        out_specs=vm,
        scratch_shapes=[
            vmem((half, width), bf16),
            vmem((n_tm, rows, cols), bf16),
            vmem((n_tm, rows, cols), bf16),
            vmem((n_tm, rows, cols), f32),
            vmem((2, up, STEPS, 8, half, 128), bf16),
            vmem((2, up, STEPS, 8, half, 128), bf16),
            vmem((STEPS, 8, half, 128), bf16),
            vmem((STEPS, 8, half, 128), bf16),
            vmem((STEPS * half, 128), bf16),
            vmem((n_tm, STEPS * half, 128), bf16),
            vmem((2, n_z, STEPS, 8, half, 128), bf16),
            vmem((2 * rows, width), bf16),
            vmem((n_z, 8, STEPS * SRC, 128), f32),
            vmem((STEPS * SRC, 16 * 128), bf16),
            vmem((n_z, 2 * rows, 16 * 128), bf16),
            vmem((STEPS, SLOTS * SRC, 2 * rows), bf16),
            vmem((STEPS, SLOTS * SRC, 128), f32),
            vmem((2 * rows, 1024), bf16),
            vmem((2 * rows, 1024), bf16),
            vmem((SLOTS * SRC, 1024), f32),
            vmem((SLOTS * SRC, 1024), f32),
            vmem((STEPS * 2 * SLOTS * 8, lags), f32),
            vmem((bins, lags), f32),
            vmem((lags, lags), bf16),
            vmem((bins, freq), bf16),
            vmem((bins, freq), bf16),
            vmem((n_tm, bins, cols), bf16),
            vmem((n_tm, bins, cols), bf16),
            vmem((n_zh, bins // n_zh, cols), f32),
            vmem((n_zh, bins // n_zh, cols), f32),
            vmem((2 * n_tm, bins // n_zh, cols), f32),
            vmem((16, lags), bf16),
            dma((1,)), dma((2,)), dma((n_tm,)), dma((n_tm,)), dma((n_tm,)), dma((n_tm,)),
            dma((2, up, 4)), dma((2, up, 4)), dma((2,)), dma((n_tm,)), dma((n_tm,)),
            dma((2, up, 4)), dma((2, up, 4)), dma((n_z,)), dma((n_z,)),
            dma((2,)), dma((n_tm,)), dma((n_tm,)), dma((n_zh,)), dma((n_zh,)), dma((2 * n_tm,)), dma((2 * n_tm,)),
        ],
        compiler_params=pltpu.CompilerParams(collective_id=0, has_side_effects=True, vmem_limit_bytes=58 * MIB),
        name="offset_stack",
    )(source_order, pos2, flat, jnp.asarray(lag_table(freq)))


def solution(mesh):
    return jax.shard_map(
        local,
        mesh=mesh,
        in_specs=(P("chan", "tm", None), P(), P()),
        out_specs=P("chan", None),
        check_vma=False,
    )
```

```python
import functools

import jax
import jax.numpy as jnp
import numpy as np
from jax import lax
from jax.experimental import pallas as pl
from jax.experimental.pallas import tpu as pltpu
from jax.sharding import PartitionSpec as P

SRC = 64
STEPS = 2
SLOTS = 12
BIN_DEV = 4
MIB = 1024 * 1024

water_level = 0.1
pair_eps = 1e-06
f32 = jnp.float32
bf16 = jnp.bfloat16


def to_bins(gap, loop, bins):
    offset = jnp.minimum(gap, loop - gap)
    return jnp.floor((offset * (2 * bins) + 0.5) * (1.0 / (loop + 1)))


def block_column(pos_ref, block):
    row = pos_ref[pl.ds(block // 2, 1), :].astype(f32)
    shape = (SRC, 2 * SRC)
    from_lane = lax.broadcasted_iota(jnp.int32, shape, 1) - lax.broadcasted_iota(jnp.int32, shape, 0)
    return jnp.sum(jnp.where(from_lane == lax.rem(block, 2) * SRC, row, 0.0), axis=1, keepdims=True)


def features(x, out, double):
    re, im = x[0::2], x[1::2]
    n = 0
    for a in range(4):
        out(n, re[a] * re[a] + im[a] * im[a])
        n += 1
    for a in range(4):
        for b in range(a + 1, 4):
            real = re[a] * re[b] + im[a] * im[b]
            imag = re[a] * im[b] - im[a] * re[b]
            if double:
                real, imag = real + real, imag + imag
            out(n, real)
            out(n + 1, imag)
            n += 2


def kernel(n_chan, n_tm, order_ref, pos_ref, x_ref, table_ref, out_ref,
           sib, part, got, inv, relay, relayed, keep, crossed, ppart, pgot, pieces,
           w2, s32, fs, fr, slots, amat, hmask, wf0, wf1, t0, t1, acc,
           place, table, mine, out0, got0, out1, got1, out2, got2, got3, xk, lag_out, lag_got,
           table_sem, share_send, share_recv, send1, recv1, send2, recv2, ring_send, ring_recv, cross_send, cross_recv,
           send3, recv3, around_send, around_recv, pass_send, pass_recv,
           swap_send, swap_recv, send4, recv4, send5, recv5, send6, recv6, lag_send, lag_recv):
    rows, width = x_ref.shape
    freq = width // 8
    cols = freq // n_tm
    half = rows // 2
    bins = BIN_DEV * n_chan
    channels = n_chan * rows
    loop = float(channels + 1 + (channels - 1) // 2)
    me_c, me = lax.axis_index("chan"), lax.axis_index("tm")
    n_z = n_chan // 4
    zh, core = me_c // 2, lax.rem(me_c, 2)
    z, hi = zh // 2, lax.rem(zh, 2)
    sibling, partner = zh * 2 + 1 - core, z * 4 + (1 - hi) * 2 + core

    def above(d):
        return lax.rem(z + d + n_z, n_z)

    ways = [above(1) * 4 + hi * 2 + core, above(-1) * 4 + hi * 2 + core]
    far = n_z // 2
    reach = [[far - (w != k) for k in range(STEPS)] for w in range(2)]
    tms = [lax.rem(me + d, n_tm) for d in range(n_tm)]
    back = [lax.rem(me - d + n_tm, n_tm) for d in range(n_tm)]
    group = [(me_c, hi, tms[d]) for d in range(1, n_tm)] + [(partner, 1 - hi, tms[d]) for d in range(n_tm)]
    group_back = [(hi, back[d]) for d in range(1, n_tm)] + [(1 - hi, back[d]) for d in range(n_tm)]

    barrier = pltpu.get_barrier_semaphore()
    for chan, _, tm in group:
        pl.semaphore_signal(barrier, inc=1, device_id={"chan": chan, "tm": tm})
    pl.semaphore_signal(barrier, inc=1, device_id={"chan": sibling, "tm": me})
    for d in range(1, n_z):
        pl.semaphore_signal(barrier, inc=1, device_id={"chan": above(d) * 4 + hi * 2 + core, "tm": me})
    load = pltpu.make_async_copy(table_ref.at[pl.ds(pl.multiple_of(core * freq, freq), freq)], table, table_sem.at[0])
    load.start()
    pl.semaphore_wait(barrier, len(group) + n_z)

    def remote(src, dst, send, recv, chan, tm):
        return pltpu.make_async_remote_copy(src_ref=src, dst_ref=dst, send_sem=send, recv_sem=recv,
                                            device_id={"chan": chan, "tm": tm})

    def share(s):
        at = pl.ds(s * 4 * freq, 4 * freq)
        return remote(x_ref.at[pl.ds(pl.multiple_of((1 - core) * half, half), half), at], sib.at[:, at],
                      share_send.at[s], share_recv.at[s], sibling, me)

    for s in range(2):
        share(s).start()
    blocks = [order_ref[k] for k in range(STEPS)]
    ahead = [lax.rem(z - blocks[k] // 4 + n_z, n_z) for k in range(STEPS)]
    own_core = [lax.rem(blocks[k], 2) == core for k in range(STEPS)]
    mine_at = pl.ds(pl.multiple_of(core * half, half), half)
    subs = [(k, s) for s in range(2) for k in range(STEPS)]

    def own(k, n, plane):
        at = pl.ds(pl.multiple_of(n * freq + plane * 128, 128), 128)
        return jnp.where(own_core[k], x_ref[mine_at, at], sib[:, at])

    def hop(w, t, k, s):
        n = pl.ds(s * 4, 4)
        return remote(relay.at[w, t, k, n], relayed.at[w, t, k, n], ring_send.at[w, t, 2 * k + s],
                      ring_recv.at[w, t, 2 * k + s], ways[w], me)

    def ring_round(t, between=()):
        for k, s in subs:
            if t == 0 and k == 0:
                share(s).wait()
            for w in range(2):
                if t >= reach[w][k]:
                    continue
                plane = above(reach[w][k] - t) if w == 0 else above(t - reach[w][k])
                if t:
                    hop(w, t - 1, k, s).wait_recv()
                for n in range(s * 4, s * 4 + 4):
                    value = own(k, n, plane)
                    if t:
                        value = jnp.where(ahead[k] == 0, value, relayed[w, t - 1, k, n])
                    relay[w, t, k, n] = value
                hop(w, t, k, s).start()
            if between:
                between.pop(0)()

    def power(first_p, last_p):
        for p in range(first_p, last_p):
            total = None
            for n in range(8):
                v = x_ref[:, n * freq + p * cols:n * freq + (p + 1) * cols].astype(f32)
                total = v * v if total is None else total + v * v
            part[p] = total

    first = [remote(part.at[tms[d]], got.at[me], send1.at[d], recv1.at[me], me_c, tms[d]) for d in range(1, n_tm)]

    def send_power():
        power(n_tm // 2, n_tm)
        for copy in first:
            copy.start()

    counts = []

    def count_pairs(k):
        src = block_column(pos_ref, blocks[k])

        def count(i, sums):
            pair_bins = to_bins(jnp.abs(src - pos_ref[pl.ds(i, 1), :].astype(f32)), loop, bins)
            rel = pair_bins - (me_c * BIN_DEV).astype(f32)
            return tuple(s + jnp.where(rel == float(b), 1.0, 0.0) for b, s in enumerate(sums))

        init = tuple(jnp.zeros((SRC, pos_ref.shape[1]), f32) for _ in range(BIN_DEV))
        counts.append(lax.fori_loop(0, pos_ref.shape[0], count, init))

    ring_round(0, [functools.partial(power, 0, n_tm // 2), send_power,
                   functools.partial(count_pairs, 0), functools.partial(count_pairs, 1)])
    factors = []
    for b in range(BIN_DEV):
        amount = sum(c[b] for c in counts)
        amount = jnp.sum(jnp.sum(amount, axis=1, keepdims=True), axis=0, keepdims=True)
        alone = jnp.where(me_c * BIN_DEV + b == 0, float(STEPS * SRC), 0.0)
        factors.append(lax.rsqrt((amount - alone) * float(n_tm * freq)))
    norm = jnp.concatenate(factors, 0)

    ring_round(1)

    lane = lax.broadcasted_iota(jnp.int32, (SRC, 2 * rows), 1)
    rec = pos_ref[pl.ds(zh, 1), :].astype(f32)
    rec = jnp.where(lane[:1] // rows == core, rec, pltpu.roll(rec, rows, axis=1))
    rec_ids = me_c * rows + lane % rows
    span = 2 * SLOTS
    col = lax.broadcasted_iota(jnp.int32, (bins, 2 * STEPS * span), 1)
    row = lax.broadcasted_iota(jnp.int32, (bins, 2 * STEPS * span), 0).astype(f32)
    inner = col % span
    marked = inner >= SLOTS
    first_bin = jnp.zeros((1, 1), f32)
    for step in range(STEPS):
        block = blocks[step]
        pair_bins = to_bins(jnp.abs(block_column(pos_ref, block) - rec), loop, bins)
        src_ids = block * SRC + lax.broadcasted_iota(jnp.int32, (SRC, 2 * rows), 0)
        lowest = jnp.min(jnp.min(pair_bins, axis=1, keepdims=True), axis=0, keepdims=True)
        first_bin = jnp.where(col < step * 2 * span, first_bin, lowest)
        rel = pair_bins - lowest
        upper = rel >= float(SLOTS)
        slot = jnp.where(upper, rel - float(SLOTS), rel)
        slots[step] = jnp.where(src_ids == rec_ids, -1.0, slot)
        for k in range(SLOTS):
            mark = jnp.max(jnp.where((slot == float(k)) & upper, 1.0, 0.0), axis=1, keepdims=True)
            hmask[step, k * SRC:(k + 1) * SRC, :] = jnp.broadcast_to(mark, (SRC, 128))
    at = first_bin + (inner - jnp.where(marked, SLOTS, 0)).astype(f32)
    lower = jnp.where(row == at, 1.0, 0.0)
    place[...] = jnp.where(marked, jnp.where(row == at + float(SLOTS), 1.0, 0.0) - lower, lower).astype(bf16)

    ring_round(2)

    total = part[me]
    for d in range(1, n_tm):
        remote(part.at[me], got.at[back[d]], send1.at[d], recv1.at[back[d]], me_c, tms[d]).wait_recv()
        total = total + got[back[d]]
    inv[me] = 1.0 / jnp.sqrt(total * (1.0 / (4 * n_tm)) + water_level)
    second = [remote(inv.at[me], inv.at[me], send2.at[d], recv2.at[me], me_c, tms[d]) for d in range(1, n_tm)]
    for copy in second:
        copy.start()

    for t in range(3, far):
        ring_round(t)

    cross = [remote(keep.at[k], crossed.at[k], cross_send.at[k], cross_recv.at[k], partner, me) for k in range(STEPS)]
    for k in range(STEPS):
        total = None
        for s in range(2):
            for w in range(2):
                hop(w, reach[w][k] - 1, k, s).wait_recv()
            for n in range(s * 4, s * 4 + 4):
                value = jnp.where(ahead[k] <= reach[0][k], relayed[0, reach[0][k] - 1, k, n],
                                  relayed[1, reach[1][k] - 1, k, n])
                value = jnp.where(ahead[k] == 0, own(k, n, z), value)
                keep[k, n] = value
                value = value.astype(f32)
                total = value * value if total is None else total + value * value
        cross[k].start()
        ppart[k * half:(k + 1) * half] = total.astype(bf16)
    spot = hi * n_tm + me
    third = [remote(ppart, pgot.at[spot], send3.at[i], recv3.at[spot], chan, tm)
             for i, (chan, _, tm) in enumerate(group)]
    for copy in third[::-1]:
        copy.start()

    def whiten(p):
        factor = inv[p]
        for n in range(8):
            at = pl.ds(pl.multiple_of(n * freq + p * cols, cols), cols)
            value = (x_ref[:, at].astype(f32) * factor).astype(bf16)
            w2[:rows, at] = value
            w2[rows:, at] = value

    whiten(me)
    for d in range(1, n_tm):
        remote(inv.at[me], inv.at[back[d]], send2.at[d], recv2.at[back[d]], me_c, tms[d]).wait_recv()
        whiten(back[d])

    def receiver_features(i, _):
        for r in range(0, rows, 16):
            x = [w2[r:r + 16, pl.ds(pl.multiple_of(n * freq + i * 128, 128), 128)].astype(f32) for n in range(8)]

            def out(n, value):
                value = value.astype(bf16)
                fr[i, r:r + 16, n * 128:(n + 1) * 128] = value
                fr[i, rows + r:rows + r + 16, n * 128:(n + 1) * 128] = value

            features(x, out, True)
        return 0

    sums = [ppart[...].astype(f32), jnp.zeros(ppart.shape, f32)]
    for i, ((chan, _, tm), (h, t)) in enumerate(zip(group, group_back)):
        other = h * n_tm + t
        remote(ppart, pgot.at[other], send3.at[i], recv3.at[other], chan, tm).wait_recv()
        side = 0 if i < n_tm - 1 else 1
        sums[side] = sums[side] + pgot[other].astype(f32)
    for k in range(STEPS):
        from_here = lax.rem(blocks[k] // 2, 2) == hi
        at = slice(k * half, (k + 1) * half)
        total = jnp.where(from_here, sums[0][at], sums[1][at])
        factor = 1.0 / jnp.sqrt(total * (1.0 / (4 * n_tm)) + water_level)
        cross[k].wait()
        for n in range(8):
            value = jnp.where(from_here, keep[k, n], crossed[k, n])
            pieces[core, z, k, n] = (value.astype(f32) * factor).astype(bf16)

    def around(w, t, k, s, arriving):
        d = t + 1 if arriving else t
        ref = pieces.at[core, above(-d) if w == 0 else above(d), k, pl.ds(s * 4, 4)]
        return remote(ref, ref, around_send.at[w, t, 2 * k + s], around_recv.at[w, t, 2 * k + s], ways[w], me)

    def pass_over(d, c):
        ref = pieces.at[c, above(d)]
        slot = d + n_z // 2
        return remote(ref, ref, pass_send.at[slot], pass_recv.at[slot], sibling, me)

    def add_energy(d, energy):
        pass_over(d, 1 - core).wait_recv()
        plane = above(d)
        for k in range(STEPS):
            for q in range(4):
                r = k * SRC + q * 16
                x = [pieces[q // 2, plane, k, n, (q % 2) * 16:(q % 2) * 16 + 16, :].astype(f32) for n in range(8)]
                for n in range(8):
                    s32[plane, n, r:r + 16, :] = x[n]

                def out(n, value):
                    fs[r:r + 16, n * 128:(n + 1) * 128] = value.astype(bf16)

                features(x, out, False)
        return energy + lax.dot_general(fs[...], fr[plane], (((1,), (1,)), ((), ())), preferred_element_type=f32)

    for k, s in subs:
        for w in range(2):
            around(w, 0, k, s, False).start()
        if (k, s) == subs[0]:
            pass_over(0, core).start()
        at = subs.index((k, s))
        lax.fori_loop(at * n_z // 4, (at + 1) * n_z // 4, receiver_features, 0)
    energy = jnp.zeros((STEPS * SRC, 2 * rows), f32)
    for t in range(1, far + 1):
        if t == far:
            energy = add_energy(1 - t, energy)
            energy = add_energy(t - 1, energy)
        for k, s in subs:
            for w in range(2):
                if t <= reach[w][k]:
                    around(w, t - 1, k, s, True).wait_recv()
                if t < reach[w][k]:
                    around(w, t, k, s, False).start()
        pass_over(-t, core).start()
        if t < far:
            pass_over(t, core).start()
            energy = add_energy(1 - t, energy)
            if t > 1:
                energy = add_energy(t - 1, energy)
    energy = add_energy(-far, energy)
    scale = lax.rsqrt(jnp.maximum(energy, 0.0) * (1.0 / (2 * freq)) + pair_eps)

    for step in range(STEPS):
        weight = scale[step * SRC:(step + 1) * SRC]
        slot = slots[step]
        for k in range(SLOTS):
            value = jnp.where(slot == float(k), weight, 0.0)
            high = value.astype(bf16).astype(f32)
            amat[step, k * SRC:(k + 1) * SRC, :] = jnp.where(lane < rows, high, value - high).astype(bf16)

    def project(step, chunk, wf, t):
        for n in range(8):
            wf[:, n * 128:(n + 1) * 128] = w2[:, pl.ds(pl.multiple_of(n * freq + chunk * 128, 128), 128)]
        t[...] = jnp.dot(amat[step], wf[...], preferred_element_type=f32)

    def gather(step, chunk, t):
        for k in range(SLOTS):
            sums = [None] * 4
            for g in range(SRC // 8):
                r = k * SRC + g * 8
                row = step * SRC + g * 8
                re, im = [], []
                for a in range(4):
                    tr = t[r:r + 8, 2 * a * 128:(2 * a + 1) * 128]
                    ti = t[r:r + 8, (2 * a + 1) * 128:(2 * a + 2) * 128]
                    sr = s32[chunk, 2 * a, row:row + 8, :]
                    si = s32[chunk, 2 * a + 1, row:row + 8, :]
                    re += [sr * tr, si * ti]
                    im.append(sr * ti - si * tr)
                real = ((re[0] + re[1]) + (re[2] + re[3])) + ((re[4] + re[5]) + (re[6] + re[7]))
                imag = (im[0] + im[1]) + (im[2] + im[3])
                mark = hmask[step, r:r + 8, :]
                new = [real, imag, real * mark, imag * mark]
                sums = new if g == 0 else [x + y for x, y in zip(sums, new)]
            for n in range(2):
                base = n * SLOTS * 8 + k * 8
                acc[step, base:base + 8, :128] = sums[2 * n]
                acc[step, base:base + 8, 128:] = sums[2 * n + 1]

    def swap(p):
        return remote(out0.at[p], got0.at[p], swap_send.at[p], swap_recv.at[p], sibling, me)

    def to_owner(p, h):
        return remote(out1.at[p, h], got1.at[spot], send4.at[p, h], recv4.at[spot], z * 4 + h * 2 + core, p)

    def to_owners(p, act):
        for h in range(2):
            @pl.when((p != me) | (hi != h))
            def _():
                act(to_owner(p, h))

    def hand_on(p):
        swap(p).wait_recv()
        value = (mine[p] + got0[p].astype(f32)).reshape(n_z, 2, 8, cols)
        for h in range(2):
            out1[p, h] = value[:, h].reshape(bins // 2, cols).astype(bf16)
        to_owners(p, lambda copy: copy.start())

    project(0, 0, wf0, t0)

    def one_chunk(p, _):
        project(1, p, wf1, t1)
        gather(0, p, t0)
        project(0, jnp.minimum(p + 1, n_tm - 1), wf0, t0)
        gather(1, p, t1)
        rows_of = []
        for step in range(STEPS):
            value = jnp.sum(acc[step].reshape(span, 8, 256), axis=1)
            high = value.astype(bf16).astype(f32)
            rows_of += [high, value - high]
        out = jnp.dot(place[...], jnp.concatenate(rows_of, 0).astype(bf16), preferred_element_type=f32)
        mine[p] = jnp.where(core == 0, out[:, :128], out[:, 128:])
        out0[p] = jnp.where(core == 0, out[:, 128:], out[:, :128]).astype(bf16)
        swap(p).start()

        @pl.when(p > 0)
        def _():
            hand_on(p - 1)

        return 0

    lax.fori_loop(0, n_tm, one_chunk, 0)
    hand_on(n_tm - 1)
    total = out1[me, hi].astype(f32)
    for (chan, _, tm), (h, t) in zip(group, group_back):
        other = h * n_tm + t
        remote(out1.at[me, hi], got1.at[other], send4.at[me, hi], recv4.at[other], chan, tm).wait_recv()
        total = total + got1[other].astype(f32)
    out2[...] = total.reshape(out2.shape)

    def to_plane(d):
        return remote(out2.at[above(d)], got2.at[z], send5.at[d], recv5.at[z], above(d) * 4 + hi * 2 + core, me)

    for d in sorted(range(1, n_z), key=lambda d: -min(d, n_z - d)):
        to_plane(d).start()
    total = out2[z]
    for d in range(1, n_z):
        other = above(-d)
        remote(out2.at[z], got2.at[other], send5.at[d], recv5.at[other], above(d) * 4 + hi * 2 + core, me).wait_recv()
        total = total + got2[other]
    got3[me] = total
    fifth = [remote(got3.at[me], got3.at[me], send6.at[d], recv6.at[me], me_c, tms[d]) for d in range(1, n_tm)]
    for copy in fifth:
        copy.start()
    for d in range(1, n_tm):
        remote(got3.at[me], got3.at[back[d]], send6.at[d], recv6.at[back[d]], me_c, tms[d]).wait_recv()
    for n in range(n_tm):
        value = got3[n]
        high = value.astype(bf16).astype(f32)
        xk[:, n * cols:(n + 1) * cols] = jnp.concatenate([high, value - high], 0).astype(bf16)
    load.wait()
    lag = 512

    def lag_swap(i):
        return remote(lag_out.at[i], lag_got.at[i], lag_send.at[i], lag_recv.at[i], sibling, me)

    for i in range(2 * freq // lag):
        both = jnp.dot(xk[...], table[:, i * lag:(i + 1) * lag], preferred_element_type=f32)
        both = both[:8] + both[8:]
        lag_out[i] = jnp.where(core == 0, both[BIN_DEV:], both[:BIN_DEV])
        lag_swap(i).start()
        out_ref[:, i * lag:(i + 1) * lag] = jnp.where(core == 0, both[:BIN_DEV], both[BIN_DEV:])
    for i in range(2 * freq // lag):
        lag_swap(i).wait_recv()
        at = slice(i * lag, (i + 1) * lag)
        out_ref[:, at] = (out_ref[:, at] + lag_got[i]) * norm

    for w in range(2):
        for k, s in subs:
            for t in range(reach[w][k]):
                hop(w, t, k, s).wait_send()
                around(w, t, k, s, False).wait_send()
    for d in range(-far, far):
        pass_over(d, core).wait_send()
    for p in range(n_tm):
        swap(p).wait_send()
        to_owners(p, lambda copy: copy.wait_send())

    for d in range(1, n_z):
        to_plane(d).wait_send()
    for i in range(2 * freq // lag):
        lag_swap(i).wait_send()
    for copy in first + second + third + fifth:
        copy.wait_send()


def lag_table(freq):
    width = 2 * freq
    phase = np.outer(np.arange(freq), np.arange(width) - freq) % width
    angle = 2.0 * np.pi / width * phase
    return np.concatenate([np.cos(angle), -np.sin(angle)], 0).astype(jnp.bfloat16)


def local(spectra, positions, source_order):
    rows, seg_dev, lags = spectra.shape
    n_chan = lax.axis_size("chan")
    n_tm = lax.axis_size("tm")
    bins = BIN_DEV * n_chan
    flat = spectra.reshape(rows, seg_dev * lags)
    pos2 = positions.reshape(n_chan // 2, 2 * rows)
    width = seg_dev * lags
    freq = lags // 2
    cols = freq // n_tm
    n_z = n_chan // 4
    half = rows // 2
    up = n_z // 2
    vm = pl.BlockSpec(memory_space=pltpu.VMEM)
    dma = pltpu.SemaphoreType.DMA
    vmem = pltpu.VMEM
    return pl.pallas_call(
        functools.partial(kernel, n_chan, n_tm),
        out_shape=jax.ShapeDtypeStruct((BIN_DEV, lags), f32),
        in_specs=[pl.BlockSpec(memory_space=pltpu.SMEM), vm, vm, pl.BlockSpec(memory_space=pl.ANY)],
        out_specs=vm,
        scratch_shapes=[
            vmem((half, width), bf16),
            vmem((n_tm, rows, cols), f32),
            vmem((n_tm, rows, cols), f32),
            vmem((n_tm, rows, cols), f32),
            vmem((2, up, STEPS, 8, half, 128), bf16),
            vmem((2, up, STEPS, 8, half, 128), bf16),
            vmem((STEPS, 8, half, 128), bf16),
            vmem((STEPS, 8, half, 128), bf16),
            vmem((STEPS * half, 128), bf16),
            vmem((2 * n_tm, STEPS * half, 128), bf16),
            vmem((2, n_z, STEPS, 8, half, 128), bf16),
            vmem((2 * rows, width), bf16),
            vmem((n_z, 8, STEPS * SRC, 128), f32),
            vmem((STEPS * SRC, 16 * 128), bf16),
            vmem((n_z, 2 * rows, 16 * 128), bf16),
            vmem((STEPS, SRC, 2 * rows), f32),
            vmem((STEPS, SLOTS * SRC, 2 * rows), bf16),
            vmem((STEPS, SLOTS * SRC, 128), f32),
            vmem((2 * rows, 1024), bf16),
            vmem((2 * rows, 1024), bf16),
            vmem((SLOTS * SRC, 1024), f32),
            vmem((SLOTS * SRC, 1024), f32),
            vmem((STEPS, 2 * SLOTS * 8, 256), f32),
            vmem((bins, 4 * STEPS * SLOTS), bf16),
            vmem((freq, lags), bf16),
            vmem((n_tm, bins, cols), f32),
            vmem((n_tm, bins, cols), bf16),
            vmem((n_tm, bins, cols), bf16),
            vmem((n_tm, 2, bins // 2, cols), bf16),
            vmem((2 * n_tm, bins // 2, cols), bf16),
            vmem((n_z, bins // n_z // 2, cols), f32),
            vmem((n_z, bins // n_z // 2, cols), f32),
            vmem((n_tm, bins // n_z // 2, cols), f32),
            vmem((16, freq), bf16),
            vmem((4, BIN_DEV, lags // 4), f32),
            vmem((4, BIN_DEV, lags // 4), f32),
            dma((1,)), dma((2,)), dma((2,)), dma((n_tm,)), dma((n_tm,)), dma((n_tm,)), dma((n_tm,)),
            dma((2, up, 4)), dma((2, up, 4)), dma((2,)), dma((2,)), dma((2 * n_tm,)), dma((2 * n_tm,)),
            dma((2, up, 4)), dma((2, up, 4)), dma((n_z,)), dma((n_z,)),
            dma((n_tm,)), dma((n_tm,)), dma((n_tm, 2)), dma((2 * n_tm,)), dma((n_z,)), dma((n_z,)),
            dma((n_tm,)), dma((n_tm,)), dma((4,)), dma((4,)),
        ],
        compiler_params=pltpu.CompilerParams(collective_id=0, has_side_effects=True, vmem_limit_bytes=58 * MIB),
        name="offset_stack",
    )(source_order, pos2, flat, jnp.asarray(lag_table(freq)))


def solution(mesh):
    return jax.shard_map(
        local,
        mesh=mesh,
        in_specs=(P("chan", "tm", None), P(), P()),
        out_specs=P("chan", None),
        check_vma=False,
    )
```

```python
import functools

import jax
import jax.numpy as jnp
import numpy as np
from jax import lax
from jax.experimental import pallas as pl
from jax.experimental.pallas import tpu as pltpu
from jax.sharding import PartitionSpec as P

SRC = 64
STEPS = 2
SLOTS = 12
BIN_DEV = 4
PARTS = 2
MIB = 1024 * 1024

water_level = 0.1
pair_eps = 1e-06
f32 = jnp.float32
bf16 = jnp.bfloat16


def to_bins(gap, loop, bins):
    offset = jnp.minimum(gap, loop - gap)
    return jnp.floor((offset * (2 * bins) + 0.5) * (1.0 / (loop + 1)))


def block_column(pos_ref, block):
    row = pos_ref[pl.ds(block // 2, 1), :].astype(f32)
    shape = (SRC, 2 * SRC)
    from_lane = lax.broadcasted_iota(jnp.int32, shape, 1) - lax.broadcasted_iota(jnp.int32, shape, 0)
    return jnp.sum(jnp.where(from_lane == lax.rem(block, 2) * SRC, row, 0.0), axis=1, keepdims=True)


def features(x, out, double):
    re, im = x[0::2], x[1::2]
    n = 0
    for a in range(4):
        out(n, re[a] * re[a] + im[a] * im[a])
        n += 1
    for a in range(4):
        for b in range(a + 1, 4):
            real = re[a] * re[b] + im[a] * im[b]
            imag = re[a] * im[b] - im[a] * re[b]
            if double:
                real, imag = real + real, imag + imag
            out(n, real)
            out(n + 1, imag)
            n += 2


def kernel(n_chan, n_tm, order_ref, pos_ref, spectra_ref, table_ref, out_ref,
           raw, x_ref, sib, part, got, inv, relay, relayed, keep, crossed, ppart, pgot, pieces,
           w2, s32, fs, fr, slots, amat, hmask, wf0, wf1, t0, t1, acc,
           place, table, mine, out0, got0, out1, got1, out2, got2, got3, xk, lag_out, lag_got,
           table_sem, raw_sem, share_send, share_recv, send1, recv1, send2, recv2, ring_send, ring_recv, cross_send, cross_recv,
           send3, recv3, around_send, around_recv, pass_send, pass_recv,
           swap_send, swap_recv, send4, recv4, send5, recv5, send6, recv6, lag_send, lag_recv):
    rows, width = x_ref.shape
    freq = width // 8
    cols = freq // n_tm
    half = rows // 2
    bins = BIN_DEV * n_chan
    channels = n_chan * rows
    loop = float(channels + 1 + (channels - 1) // 2)
    me_c, me = lax.axis_index("chan"), lax.axis_index("tm")
    n_z = n_chan // 4
    zh, core = me_c // 2, lax.rem(me_c, 2)
    z, hi = zh // 2, lax.rem(zh, 2)
    sibling, partner = zh * 2 + 1 - core, z * 4 + (1 - hi) * 2 + core

    def above(d):
        return lax.rem(z + d + n_z, n_z)

    ways = [above(1) * 4 + hi * 2 + core, above(-1) * 4 + hi * 2 + core]
    far = n_z // 2
    reach = [[far - (w != k) for k in range(STEPS)] for w in range(2)]
    tms = [lax.rem(me + d, n_tm) for d in range(n_tm)]
    back = [lax.rem(me - d + n_tm, n_tm) for d in range(n_tm)]
    group = [(me_c, hi, tms[d]) for d in range(1, n_tm)] + [(partner, 1 - hi, tms[d]) for d in range(n_tm)]
    group_back = [(hi, back[d]) for d in range(1, n_tm)] + [(1 - hi, back[d]) for d in range(n_tm)]

    barrier = pltpu.get_barrier_semaphore()
    for chan, _, tm in group:
        pl.semaphore_signal(barrier, inc=1, device_id={"chan": chan, "tm": tm})
    pl.semaphore_signal(barrier, inc=1, device_id={"chan": sibling, "tm": me})
    for d in range(1, n_z):
        pl.semaphore_signal(barrier, inc=1, device_id={"chan": above(d) * 4 + hi * 2 + core, "tm": me})
    load = pltpu.make_async_copy(table_ref.at[pl.ds(pl.multiple_of(core * freq, freq), freq)], table, table_sem.at[0])
    fetch = pltpu.make_async_copy(spectra_ref, raw, raw_sem.at[0])
    fetch.start()
    fetch.wait()
    load.start()
    lags = raw.shape[2]
    for a in range(raw.shape[1]):
        x_ref[:, a * lags:(a + 1) * lags] = raw[:, a, :]
    pl.semaphore_wait(barrier, len(group) + n_z)

    def remote(src, dst, send, recv, chan, tm):
        return pltpu.make_async_remote_copy(src_ref=src, dst_ref=dst, send_sem=send, recv_sem=recv,
                                            device_id={"chan": chan, "tm": tm})

    def share(s):
        at = pl.ds(s * 4 * freq, 4 * freq)
        return remote(x_ref.at[pl.ds(pl.multiple_of((1 - core) * half, half), half), at], sib.at[:, at],
                      share_send.at[s], share_recv.at[s], sibling, me)

    for s in range(2):
        share(s).start()
    blocks = [order_ref[k] for k in range(STEPS)]
    ahead = [lax.rem(z - blocks[k] // 4 + n_z, n_z) for k in range(STEPS)]
    own_core = [lax.rem(blocks[k], 2) == core for k in range(STEPS)]
    mine_at = pl.ds(pl.multiple_of(core * half, half), half)
    subs = [(k, s) for s in range(PARTS) for k in range(STEPS)]
    per = 8 // PARTS

    def own(k, n, plane):
        at = pl.ds(pl.multiple_of(n * freq + plane * 128, 128), 128)
        return jnp.where(own_core[k], x_ref[mine_at, at], sib[:, at])

    def hop(w, t, k, s):
        n = pl.ds(s * per, per)
        return remote(relay.at[w, t, k, n], relayed.at[w, t, k, n], ring_send.at[w, t, k * PARTS + s],
                      ring_recv.at[w, t, k * PARTS + s], ways[w], me)

    def ring_round(t, between=()):
        for k, s in subs:
            if t == 0 and k == 0 and s % (PARTS // 2) == 0:
                share(s // (PARTS // 2)).wait()
            for w in range(2):
                if t >= reach[w][k]:
                    continue
                plane = above(reach[w][k] - t) if w == 0 else above(t - reach[w][k])
                if t:
                    hop(w, t - 1, k, s).wait_recv()
                for n in range(s * per, (s + 1) * per):
                    value = own(k, n, plane)
                    if t:
                        value = jnp.where(ahead[k] == 0, value, relayed[w, t - 1, k, n])
                    relay[w, t, k, n] = value
                hop(w, t, k, s).start()
            if between:
                between.pop(0)()

    def power(first_p, last_p):
        for p in range(first_p, last_p):
            total = None
            for n in range(8):
                v = x_ref[:, n * freq + p * cols:n * freq + (p + 1) * cols].astype(f32)
                total = v * v if total is None else total + v * v
            part[p] = total

    first = [remote(part.at[tms[d]], got.at[me], send1.at[d], recv1.at[me], me_c, tms[d]) for d in range(1, n_tm)]

    counts = []

    def count_pairs(k):
        src = block_column(pos_ref, blocks[k])

        def count(i, sums):
            pair_bins = to_bins(jnp.abs(src - pos_ref[pl.ds(i, 1), :].astype(f32)), loop, bins)
            rel = pair_bins - (me_c * BIN_DEV).astype(f32)
            return tuple(s + jnp.where(rel == float(b), 1.0, 0.0) for b, s in enumerate(sums))

        init = tuple(jnp.zeros((SRC, pos_ref.shape[1]), f32) for _ in range(BIN_DEV))
        counts.append(lax.fori_loop(0, pos_ref.shape[0], count, init))

    step = n_tm // len(subs)
    ring_round(0, [functools.partial(power, i * step, (i + 1) * step) for i in range(len(subs))])
    for copy in first:
        copy.start()
    for k in range(STEPS):
        count_pairs(k)
    factors = []
    for b in range(BIN_DEV):
        amount = sum(c[b] for c in counts)
        amount = jnp.sum(jnp.sum(amount, axis=1, keepdims=True), axis=0, keepdims=True)
        alone = jnp.where(me_c * BIN_DEV + b == 0, float(STEPS * SRC), 0.0)
        factors.append(lax.rsqrt((amount - alone) * float(n_tm * freq)))
    norm = jnp.concatenate(factors, 0)

    ring_round(1)

    lane = lax.broadcasted_iota(jnp.int32, (SRC, 2 * rows), 1)
    rec = pos_ref[pl.ds(zh, 1), :].astype(f32)
    rec = jnp.where(lane[:1] // rows == core, rec, pltpu.roll(rec, rows, axis=1))
    rec_ids = me_c * rows + lane % rows
    span = 2 * SLOTS
    col = lax.broadcasted_iota(jnp.int32, (bins, 2 * STEPS * span), 1)
    row = lax.broadcasted_iota(jnp.int32, (bins, 2 * STEPS * span), 0).astype(f32)
    inner = col % span
    marked = inner >= SLOTS
    first_bin = jnp.zeros((1, 1), f32)
    for step in range(STEPS):
        block = blocks[step]
        pair_bins = to_bins(jnp.abs(block_column(pos_ref, block) - rec), loop, bins)
        src_ids = block * SRC + lax.broadcasted_iota(jnp.int32, (SRC, 2 * rows), 0)
        lowest = jnp.min(jnp.min(pair_bins, axis=1, keepdims=True), axis=0, keepdims=True)
        first_bin = jnp.where(col < step * 2 * span, first_bin, lowest)
        rel = pair_bins - lowest
        upper = rel >= float(SLOTS)
        slot = jnp.where(upper, rel - float(SLOTS), rel)
        slots[step] = jnp.where(src_ids == rec_ids, -1.0, slot)
        for k in range(SLOTS):
            mark = jnp.max(jnp.where((slot == float(k)) & upper, 1.0, 0.0), axis=1, keepdims=True)
            hmask[step, k * SRC:(k + 1) * SRC, :] = jnp.broadcast_to(mark, (SRC, 128))
    at = first_bin + (inner - jnp.where(marked, SLOTS, 0)).astype(f32)
    lower = jnp.where(row == at, 1.0, 0.0)
    place[...] = jnp.where(marked, jnp.where(row == at + float(SLOTS), 1.0, 0.0) - lower, lower).astype(bf16)

    ring_round(2)

    total = part[me]
    for d in range(1, n_tm):
        remote(part.at[me], got.at[back[d]], send1.at[d], recv1.at[back[d]], me_c, tms[d]).wait_recv()
        total = total + got[back[d]]
    inv[me] = 1.0 / jnp.sqrt(total * (1.0 / (4 * n_tm)) + water_level)
    second = [remote(inv.at[me], inv.at[me], send2.at[d], recv2.at[me], me_c, tms[d]) for d in range(1, n_tm)]
    for copy in second:
        copy.start()

    for t in range(3, far):
        ring_round(t)

    cross = [remote(keep.at[k], crossed.at[k], cross_send.at[k], cross_recv.at[k], partner, me) for k in range(STEPS)]
    for k in range(STEPS):
        total = None
        for s in range(PARTS):
            for w in range(2):
                hop(w, reach[w][k] - 1, k, s).wait_recv()
            for n in range(s * per, (s + 1) * per):
                value = jnp.where(ahead[k] <= reach[0][k], relayed[0, reach[0][k] - 1, k, n],
                                  relayed[1, reach[1][k] - 1, k, n])
                value = jnp.where(ahead[k] == 0, own(k, n, z), value)
                keep[k, n] = value
                value = value.astype(f32)
                total = value * value if total is None else total + value * value
        cross[k].start()
        ppart[k * half:(k + 1) * half] = total.astype(bf16)
    spot = hi * n_tm + me
    third = [remote(ppart, pgot.at[spot], send3.at[i], recv3.at[spot], chan, tm)
             for i, (chan, _, tm) in enumerate(group)]
    for copy in third[::-1]:
        copy.start()

    def whiten(p):
        factor = inv[p]
        for n in range(8):
            at = pl.ds(pl.multiple_of(n * freq + p * cols, cols), cols)
            value = (x_ref[:, at].astype(f32) * factor).astype(bf16)
            w2[:rows, at] = value
            w2[rows:, at] = value

    whiten(me)
    for d in range(1, n_tm):
        remote(inv.at[me], inv.at[back[d]], send2.at[d], recv2.at[back[d]], me_c, tms[d]).wait_recv()
        whiten(back[d])

    def receiver_features(i, _):
        for r in range(0, rows, 16):
            x = [w2[r:r + 16, pl.ds(pl.multiple_of(n * freq + i * 128, 128), 128)].astype(f32) for n in range(8)]

            def out(n, value):
                value = value.astype(bf16)
                fr[i, r:r + 16, n * 128:(n + 1) * 128] = value
                fr[i, rows + r:rows + r + 16, n * 128:(n + 1) * 128] = value

            features(x, out, True)
        return 0

    sums = [ppart[...].astype(f32), jnp.zeros(ppart.shape, f32)]
    for i, ((chan, _, tm), (h, t)) in enumerate(zip(group, group_back)):
        other = h * n_tm + t
        remote(ppart, pgot.at[other], send3.at[i], recv3.at[other], chan, tm).wait_recv()
        side = 0 if i < n_tm - 1 else 1
        sums[side] = sums[side] + pgot[other].astype(f32)
    for k in range(STEPS):
        from_here = lax.rem(blocks[k] // 2, 2) == hi
        at = slice(k * half, (k + 1) * half)
        total = jnp.where(from_here, sums[0][at], sums[1][at])
        factor = 1.0 / jnp.sqrt(total * (1.0 / (4 * n_tm)) + water_level)
        cross[k].wait()
        for n in range(8):
            value = jnp.where(from_here, keep[k, n], crossed[k, n])
            pieces[core, z, k, n] = (value.astype(f32) * factor).astype(bf16)

    def around(w, t, k, s, arriving):
        d = t + 1 if arriving else t
        ref = pieces.at[core, above(-d) if w == 0 else above(d), k, pl.ds(s * per, per)]
        return remote(ref, ref, around_send.at[w, t, k * PARTS + s], around_recv.at[w, t, k * PARTS + s], ways[w], me)

    def pass_over(d, c):
        ref = pieces.at[c, above(d)]
        slot = d + n_z // 2
        return remote(ref, ref, pass_send.at[slot], pass_recv.at[slot], sibling, me)

    def add_energy(d, energy):
        pass_over(d, 1 - core).wait_recv()
        plane = above(d)
        for k in range(STEPS):
            for q in range(4):
                r = k * SRC + q * 16
                x = [pieces[q // 2, plane, k, n, (q % 2) * 16:(q % 2) * 16 + 16, :].astype(f32) for n in range(8)]
                for n in range(8):
                    s32[plane, n, r:r + 16, :] = x[n]

                def out(n, value):
                    fs[r:r + 16, n * 128:(n + 1) * 128] = value.astype(bf16)

                features(x, out, False)
        return energy + lax.dot_general(fs[...], fr[plane], (((1,), (1,)), ((), ())), preferred_element_type=f32)

    for k, s in subs:
        for w in range(2):
            around(w, 0, k, s, False).start()
        if (k, s) == subs[0]:
            pass_over(0, core).start()
        at = subs.index((k, s))
        lax.fori_loop(at * n_z // len(subs), (at + 1) * n_z // len(subs), receiver_features, 0)
    energy = jnp.zeros((STEPS * SRC, 2 * rows), f32)
    for t in range(1, far + 1):
        if t == far:
            energy = add_energy(1 - t, energy)
            energy = add_energy(t - 1, energy)
        for k, s in subs:
            for w in range(2):
                if t <= reach[w][k]:
                    around(w, t - 1, k, s, True).wait_recv()
                if t < reach[w][k]:
                    around(w, t, k, s, False).start()
        pass_over(-t, core).start()
        if t < far:
            pass_over(t, core).start()
            energy = add_energy(1 - t, energy)
            if t > 1:
                energy = add_energy(t - 1, energy)
    energy = add_energy(-far, energy)
    scale = lax.rsqrt(jnp.maximum(energy, 0.0) * (1.0 / (2 * freq)) + pair_eps)

    def weigh(step):
        weight = scale[step * SRC:(step + 1) * SRC]
        slot = slots[step]
        for k in range(SLOTS):
            value = jnp.where(slot == float(k), weight, 0.0)
            high = value.astype(bf16).astype(f32)
            amat[step, k * SRC:(k + 1) * SRC, :] = jnp.where(lane < rows, high, value - high).astype(bf16)

    def project(step, chunk, wf, t):
        for n in range(8):
            wf[:, n * 128:(n + 1) * 128] = w2[:, pl.ds(pl.multiple_of(n * freq + chunk * 128, 128), 128)]
        t[...] = jnp.dot(amat[step], wf[...], preferred_element_type=f32)

    def gather(step, chunk, t):
        for k in range(SLOTS):
            sums = [None] * 4
            for g in range(SRC // 8):
                r = k * SRC + g * 8
                row = step * SRC + g * 8
                re, im = [], []
                for a in range(4):
                    tr = t[r:r + 8, 2 * a * 128:(2 * a + 1) * 128]
                    ti = t[r:r + 8, (2 * a + 1) * 128:(2 * a + 2) * 128]
                    sr = s32[chunk, 2 * a, row:row + 8, :]
                    si = s32[chunk, 2 * a + 1, row:row + 8, :]
                    re += [sr * tr, si * ti]
                    im.append(sr * ti - si * tr)
                real = ((re[0] + re[1]) + (re[2] + re[3])) + ((re[4] + re[5]) + (re[6] + re[7]))
                imag = (im[0] + im[1]) + (im[2] + im[3])
                mark = hmask[step, r:r + 8, :]
                new = [real, imag, real * mark, imag * mark]
                sums = new if g == 0 else [x + y for x, y in zip(sums, new)]
            for n in range(2):
                base = n * SLOTS * 8 + k * 8
                acc[step, base:base + 8, :128] = sums[2 * n]
                acc[step, base:base + 8, 128:] = sums[2 * n + 1]

    def swap(p):
        return remote(out0.at[p], got0.at[p], swap_send.at[p], swap_recv.at[p], sibling, me)

    def to_owner(p, h):
        return remote(out1.at[p, h], got1.at[spot], send4.at[p, h], recv4.at[spot], z * 4 + h * 2 + core, p)

    def to_owners(p, act):
        for h in range(2):
            @pl.when((p != me) | (hi != h))
            def _():
                act(to_owner(p, h))

    def hand_on(p):
        swap(p).wait_recv()
        value = (mine[p] + got0[p].astype(f32)).reshape(n_z, 2, 8, cols)
        for h in range(2):
            out1[p, h] = value[:, h].reshape(bins // 2, cols).astype(bf16)
        to_owners(p, lambda copy: copy.start())

    def chunk(q):
        return lax.rem(me + 1 + q, n_tm)

    weigh(0)
    project(0, chunk(0), wf0, t0)
    weigh(1)

    def one_chunk(q, _):
        p = chunk(q)
        project(1, p, wf1, t1)
        gather(0, p, t0)
        project(0, chunk(q + 1), wf0, t0)
        gather(1, p, t1)
        rows_of = []
        for step in range(STEPS):
            value = jnp.sum(acc[step].reshape(span, 8, 256), axis=1)
            high = value.astype(bf16).astype(f32)
            rows_of += [high, value - high]
        out = jnp.dot(place[...], jnp.concatenate(rows_of, 0).astype(bf16), preferred_element_type=f32)
        mine[p] = jnp.where(core == 0, out[:, :128], out[:, 128:])
        out0[p] = jnp.where(core == 0, out[:, 128:], out[:, :128]).astype(bf16)
        swap(p).start()

        @pl.when(q > 0)
        def _():
            hand_on(chunk(q - 1))

        return 0

    lax.fori_loop(0, n_tm, one_chunk, 0)
    hand_on(me)
    total = out1[me, hi].astype(f32)
    for (chan, _, tm), (h, t) in zip(group, group_back):
        other = h * n_tm + t
        remote(out1.at[me, hi], got1.at[other], send4.at[me, hi], recv4.at[other], chan, tm).wait_recv()
        total = total + got1[other].astype(f32)
    out2[...] = total.reshape(out2.shape)

    def to_plane(d):
        return remote(out2.at[above(d)], got2.at[z], send5.at[d], recv5.at[z], above(d) * 4 + hi * 2 + core, me)

    for d in sorted(range(1, n_z), key=lambda d: -min(d, n_z - d)):
        to_plane(d).start()
    total = out2[z]
    for d in range(1, n_z):
        other = above(-d)
        remote(out2.at[z], got2.at[other], send5.at[d], recv5.at[other], above(d) * 4 + hi * 2 + core, me).wait_recv()
        total = total + got2[other]
    got3[me] = total
    fifth = [remote(got3.at[me], got3.at[me], send6.at[d], recv6.at[me], me_c, tms[d]) for d in range(1, n_tm)]
    for copy in fifth:
        copy.start()
    for d in range(1, n_tm):
        remote(got3.at[me], got3.at[back[d]], send6.at[d], recv6.at[back[d]], me_c, tms[d]).wait_recv()
    for n in range(n_tm):
        value = got3[n]
        high = value.astype(bf16).astype(f32)
        xk[:, n * cols:(n + 1) * cols] = jnp.concatenate([high, value - high], 0).astype(bf16)
    load.wait()
    lag = 512

    def lag_swap(i):
        return remote(lag_out.at[i], lag_got.at[i], lag_send.at[i], lag_recv.at[i], sibling, me)

    for i in range(2 * freq // lag):
        both = jnp.dot(xk[...], table[:, i * lag:(i + 1) * lag], preferred_element_type=f32)
        both = both[:8] + both[8:]
        lag_out[i] = jnp.where(core == 0, both[BIN_DEV:], both[:BIN_DEV])
        lag_swap(i).start()
        out_ref[:, i * lag:(i + 1) * lag] = jnp.where(core == 0, both[:BIN_DEV], both[BIN_DEV:])
    for i in range(2 * freq // lag):
        lag_swap(i).wait_recv()
        at = slice(i * lag, (i + 1) * lag)
        out_ref[:, at] = (out_ref[:, at] + lag_got[i]) * norm

    for w in range(2):
        for k, s in subs:
            for t in range(reach[w][k]):
                hop(w, t, k, s).wait_send()
                around(w, t, k, s, False).wait_send()
    for d in range(-far, far):
        pass_over(d, core).wait_send()
    for p in range(n_tm):
        swap(p).wait_send()
        to_owners(p, lambda copy: copy.wait_send())

    for d in range(1, n_z):
        to_plane(d).wait_send()
    for i in range(2 * freq // lag):
        lag_swap(i).wait_send()
    for copy in first + second + third + fifth:
        copy.wait_send()


def lag_table(freq):
    width = 2 * freq
    phase = np.outer(np.arange(freq), np.arange(width) - freq) % width
    angle = 2.0 * np.pi / width * phase
    return np.concatenate([np.cos(angle), -np.sin(angle)], 0).astype(jnp.bfloat16)


def local(spectra, positions, source_order):
    rows, seg_dev, lags = spectra.shape
    n_chan = lax.axis_size("chan")
    n_tm = lax.axis_size("tm")
    bins = BIN_DEV * n_chan
    pos2 = positions.reshape(n_chan // 2, 2 * rows)
    width = seg_dev * lags
    freq = lags // 2
    cols = freq // n_tm
    n_z = n_chan // 4
    half = rows // 2
    up = n_z // 2
    vm = pl.BlockSpec(memory_space=pltpu.VMEM)
    hbm = pl.BlockSpec(memory_space=pl.ANY)
    dma = pltpu.SemaphoreType.DMA
    vmem = pltpu.VMEM
    return pl.pallas_call(
        functools.partial(kernel, n_chan, n_tm),
        out_shape=jax.ShapeDtypeStruct((BIN_DEV, lags), f32),
        in_specs=[pl.BlockSpec(memory_space=pltpu.SMEM), vm, hbm, hbm],
        out_specs=vm,
        scratch_shapes=[
            vmem((rows, seg_dev, lags), bf16),
            vmem((rows, width), bf16),
            vmem((half, width), bf16),
            vmem((n_tm, rows, cols), f32),
            vmem((n_tm, rows, cols), f32),
            vmem((n_tm, rows, cols), f32),
            vmem((2, up, STEPS, 8, half, 128), bf16),
            vmem((2, up, STEPS, 8, half, 128), bf16),
            vmem((STEPS, 8, half, 128), bf16),
            vmem((STEPS, 8, half, 128), bf16),
            vmem((STEPS * half, 128), bf16),
            vmem((2 * n_tm, STEPS * half, 128), bf16),
            vmem((2, n_z, STEPS, 8, half, 128), bf16),
            vmem((2 * rows, width), bf16),
            vmem((n_z, 8, STEPS * SRC, 128), f32),
            vmem((STEPS * SRC, 16 * 128), bf16),
            vmem((n_z, 2 * rows, 16 * 128), bf16),
            vmem((STEPS, SRC, 2 * rows), f32),
            vmem((STEPS, SLOTS * SRC, 2 * rows), bf16),
            vmem((STEPS, SLOTS * SRC, 128), f32),
            vmem((2 * rows, 1024), bf16),
            vmem((2 * rows, 1024), bf16),
            vmem((SLOTS * SRC, 1024), f32),
            vmem((SLOTS * SRC, 1024), f32),
            vmem((STEPS, 2 * SLOTS * 8, 256), f32),
            vmem((bins, 4 * STEPS * SLOTS), bf16),
            vmem((freq, lags), bf16),
            vmem((n_tm, bins, cols), f32),
            vmem((n_tm, bins, cols), bf16),
            vmem((n_tm, bins, cols), bf16),
            vmem((n_tm, 2, bins // 2, cols), bf16),
            vmem((2 * n_tm, bins // 2, cols), bf16),
            vmem((n_z, bins // n_z // 2, cols), f32),
            vmem((n_z, bins // n_z // 2, cols), f32),
            vmem((n_tm, bins // n_z // 2, cols), f32),
            vmem((16, freq), bf16),
            vmem((4, BIN_DEV, lags // 4), f32),
            vmem((4, BIN_DEV, lags // 4), f32),
            dma((1,)), dma((1,)), dma((2,)), dma((2,)), dma((n_tm,)), dma((n_tm,)), dma((n_tm,)), dma((n_tm,)),
            dma((2, up, STEPS * PARTS)), dma((2, up, STEPS * PARTS)), dma((2,)), dma((2,)), dma((2 * n_tm,)), dma((2 * n_tm,)),
            dma((2, up, STEPS * PARTS)), dma((2, up, STEPS * PARTS)), dma((n_z,)), dma((n_z,)),
            dma((n_tm,)), dma((n_tm,)), dma((n_tm, 2)), dma((2 * n_tm,)), dma((n_z,)), dma((n_z,)),
            dma((n_tm,)), dma((n_tm,)), dma((4,)), dma((4,)),
        ],
        compiler_params=pltpu.CompilerParams(collective_id=0, has_side_effects=True, vmem_limit_bytes=58 * MIB),
        name="offset_stack",
    )(source_order, pos2, spectra, jnp.asarray(lag_table(freq)))


def solution(mesh):
    return jax.shard_map(
        local,
        mesh=mesh,
        in_specs=(P("chan", "tm", None), P(), P()),
        out_specs=P("chan", None),
        check_vma=False,
    )
```

```python
import functools

import jax
import jax.numpy as jnp
import numpy as np
from jax import lax
from jax.experimental import pallas as pl
from jax.experimental.pallas import tpu as pltpu
from jax.sharding import PartitionSpec as P

SRC = 64
STEPS = 2
SLOTS = 12
BIN_DEV = 4
PARTS = 2
MIB = 1024 * 1024

water_level = 0.1
pair_eps = 1e-06
f32 = jnp.float32
bf16 = jnp.bfloat16


def to_bins(gap, loop, bins):
    offset = jnp.minimum(gap, loop - gap)
    return jnp.floor((offset * (2 * bins) + 0.5) * (1.0 / (loop + 1)))


def block_column(pos_ref, block):
    row = pos_ref[pl.ds(block // 2, 1), :].astype(f32)
    shape = (SRC, 2 * SRC)
    from_lane = lax.broadcasted_iota(jnp.int32, shape, 1) - lax.broadcasted_iota(jnp.int32, shape, 0)
    return jnp.sum(jnp.where(from_lane == lax.rem(block, 2) * SRC, row, 0.0), axis=1, keepdims=True)


def features(x, out, double):
    re, im = x[0::2], x[1::2]
    n = 0
    for a in range(4):
        out(n, re[a] * re[a] + im[a] * im[a])
        n += 1
    for a in range(4):
        for b in range(a + 1, 4):
            real = re[a] * re[b] + im[a] * im[b]
            imag = re[a] * im[b] - im[a] * re[b]
            if double:
                real, imag = real + real, imag + imag
            out(n, real)
            out(n + 1, imag)
            n += 2


def kernel(n_chan, n_tm, order_ref, pos_ref, spectra_ref, table_ref, out_ref,
           raw, x_ref, sib, part, got, inv, relay, relayed, keep, crossed, ppart, pgot, pieces,
           w2, s32, fs, fr, slots, amat, hmask, wf0, wf1, t0, t1, acc,
           place, table, mine, out0, got0, out1, got1, last_out, last_got, out2, got2, got3, xk, lag_out, lag_got,
           table_sem, raw_sem, share_send, share_recv, send1, recv1, send2, recv2, ring_send, ring_recv, cross_send, cross_recv,
           send3, recv3, around_send, around_recv, pass_send, pass_recv,
           swap_send, swap_recv, send4, recv4, send5, recv5, last_send, last_recv, send6, recv6, lag_send, lag_recv):
    rows, width = x_ref.shape
    freq = width // 8
    cols = freq // n_tm
    half = rows // 2
    bins = BIN_DEV * n_chan
    channels = n_chan * rows
    loop = float(channels + 1 + (channels - 1) // 2)
    me_c, me = lax.axis_index("chan"), lax.axis_index("tm")
    n_z = n_chan // 4
    zh, core = me_c // 2, lax.rem(me_c, 2)
    z, hi = zh // 2, lax.rem(zh, 2)
    sibling, partner = zh * 2 + 1 - core, z * 4 + (1 - hi) * 2 + core

    def above(d):
        return lax.rem(z + d + n_z, n_z)

    ways = [above(1) * 4 + hi * 2 + core, above(-1) * 4 + hi * 2 + core]
    far = n_z // 2
    reach = [[far - (w != k) for k in range(STEPS)] for w in range(2)]
    tms = [lax.rem(me + d, n_tm) for d in range(n_tm)]
    back = [lax.rem(me - d + n_tm, n_tm) for d in range(n_tm)]
    group = [(me_c, hi, tms[d]) for d in range(1, n_tm)] + [(partner, 1 - hi, tms[d]) for d in range(n_tm)]
    group_back = [(hi, back[d]) for d in range(1, n_tm)] + [(1 - hi, back[d]) for d in range(n_tm)]

    barrier = pltpu.get_barrier_semaphore()
    for chan, _, tm in group:
        pl.semaphore_signal(barrier, inc=1, device_id={"chan": chan, "tm": tm})
    across = z * 4 + (1 - hi) * 2 + 1 - core
    for chan in (sibling, across):
        pl.semaphore_signal(barrier, inc=1, device_id={"chan": chan, "tm": me})
    for d in range(1, n_z):
        pl.semaphore_signal(barrier, inc=1, device_id={"chan": above(d) * 4 + hi * 2 + core, "tm": me})
    load = pltpu.make_async_copy(table_ref.at[pl.ds(pl.multiple_of(core * freq, freq), freq)], table, table_sem.at[0])
    fetch = pltpu.make_async_copy(spectra_ref, raw, raw_sem.at[0])
    fetch.start()
    fetch.wait()
    load.start()
    lags = raw.shape[2]
    for a in range(raw.shape[1]):
        x_ref[:, a * lags:(a + 1) * lags] = raw[:, a, :]
    pl.semaphore_wait(barrier, len(group) + n_z + 1)

    def remote(src, dst, send, recv, chan, tm):
        return pltpu.make_async_remote_copy(src_ref=src, dst_ref=dst, send_sem=send, recv_sem=recv,
                                            device_id={"chan": chan, "tm": tm})

    def share(s):
        at = pl.ds(s * 4 * freq, 4 * freq)
        return remote(x_ref.at[pl.ds(pl.multiple_of((1 - core) * half, half), half), at], sib.at[:, at],
                      share_send.at[s], share_recv.at[s], sibling, me)

    share(0).start()
    blocks = [order_ref[k] for k in range(STEPS)]
    ahead = [lax.rem(z - blocks[k] // 4 + n_z, n_z) for k in range(STEPS)]
    own_core = [lax.rem(blocks[k], 2) == core for k in range(STEPS)]
    mine_at = pl.ds(pl.multiple_of(core * half, half), half)
    subs = [(k, s) for s in range(PARTS) for k in range(STEPS)]
    per = 8 // PARTS

    def own(k, n, plane):
        at = pl.ds(pl.multiple_of(n * freq + plane * 128, 128), 128)
        return jnp.where(own_core[k], x_ref[mine_at, at], sib[:, at])

    def hop(w, t, k, s):
        n = pl.ds(s * per, per)
        return remote(relay.at[w, t, k, n], relayed.at[w, t, k, n], ring_send.at[w, t, k * PARTS + s],
                      ring_recv.at[w, t, k * PARTS + s], ways[w], me)

    def ring_round(t, between=()):
        for k, s in subs:
            if t == 0 and k == 0 and s % (PARTS // 2) == 0:
                share(s // (PARTS // 2)).wait()
                if s == 0:
                    share(1).start()
            for w in range(2):
                if t >= reach[w][k]:
                    continue
                plane = above(reach[w][k] - t) if w == 0 else above(t - reach[w][k])
                if t:
                    hop(w, t - 1, k, s).wait_recv()
                for n in range(s * per, (s + 1) * per):
                    value = own(k, n, plane)
                    if t:
                        value = jnp.where(ahead[k] == 0, value, relayed[w, t - 1, k, n])
                    relay[w, t, k, n] = value
                hop(w, t, k, s).start()
            if between:
                between.pop(0)()

    def power(first_p, last_p):
        for p in range(first_p, last_p):
            total = None
            for n in range(8):
                v = x_ref[:, n * freq + p * cols:n * freq + (p + 1) * cols].astype(f32)
                total = v * v if total is None else total + v * v
            part[p] = total

    first = [remote(part.at[tms[d]], got.at[me], send1.at[d], recv1.at[me], me_c, tms[d]) for d in range(1, n_tm)]

    counts = []

    def count_pairs(k):
        src = block_column(pos_ref, blocks[k])

        def count(i, sums):
            pair_bins = to_bins(jnp.abs(src - pos_ref[pl.ds(i, 1), :].astype(f32)), loop, bins)
            rel = pair_bins - (me_c * BIN_DEV).astype(f32)
            return tuple(s + jnp.where(rel == float(b), 1.0, 0.0) for b, s in enumerate(sums))

        init = tuple(jnp.zeros((SRC, pos_ref.shape[1]), f32) for _ in range(BIN_DEV))
        counts.append(lax.fori_loop(0, pos_ref.shape[0], count, init))

    step = n_tm // len(subs)
    ring_round(0, [functools.partial(power, i * step, (i + 1) * step) for i in range(len(subs))])
    for copy in first:
        copy.start()
    for k in range(STEPS):
        count_pairs(k)
    factors = []
    for b in range(BIN_DEV):
        amount = sum(c[b] for c in counts)
        amount = jnp.sum(jnp.sum(amount, axis=1, keepdims=True), axis=0, keepdims=True)
        alone = jnp.where(me_c * BIN_DEV + b == 0, float(STEPS * SRC), 0.0)
        factors.append(lax.rsqrt((amount - alone) * float(n_tm * freq)))
    norm = jnp.concatenate(factors, 0)

    ring_round(1)

    lane = lax.broadcasted_iota(jnp.int32, (SRC, 2 * rows), 1)
    rec = pos_ref[pl.ds(zh, 1), :].astype(f32)
    rec = jnp.where(lane[:1] // rows == core, rec, pltpu.roll(rec, rows, axis=1))
    rec_ids = me_c * rows + lane % rows
    span = 2 * SLOTS
    col = lax.broadcasted_iota(jnp.int32, (bins, 2 * STEPS * span), 1)
    row = lax.broadcasted_iota(jnp.int32, (bins, 2 * STEPS * span), 0).astype(f32)
    inner = col % span
    marked = inner >= SLOTS
    first_bin = jnp.zeros((1, 1), f32)
    for step in range(STEPS):
        block = blocks[step]
        pair_bins = to_bins(jnp.abs(block_column(pos_ref, block) - rec), loop, bins)
        src_ids = block * SRC + lax.broadcasted_iota(jnp.int32, (SRC, 2 * rows), 0)
        lowest = jnp.min(jnp.min(pair_bins, axis=1, keepdims=True), axis=0, keepdims=True)
        first_bin = jnp.where(col < step * 2 * span, first_bin, lowest)
        rel = pair_bins - lowest
        upper = rel >= float(SLOTS)
        slot = jnp.where(upper, rel - float(SLOTS), rel)
        slots[step] = jnp.where(src_ids == rec_ids, -1.0, slot)
        for k in range(SLOTS):
            mark = jnp.max(jnp.where((slot == float(k)) & upper, 1.0, 0.0), axis=1, keepdims=True)
            hmask[step, k * SRC:(k + 1) * SRC, :] = jnp.broadcast_to(mark, (SRC, 128))
    at = first_bin + (inner - jnp.where(marked, SLOTS, 0)).astype(f32)
    lower = jnp.where(row == at, 1.0, 0.0)
    place[...] = jnp.where(marked, jnp.where(row == at + float(SLOTS), 1.0, 0.0) - lower, lower).astype(bf16)

    ring_round(2)

    total = part[me]
    for d in range(1, n_tm):
        remote(part.at[me], got.at[back[d]], send1.at[d], recv1.at[back[d]], me_c, tms[d]).wait_recv()
        total = total + got[back[d]]
    inv[me] = 1.0 / jnp.sqrt(total * (1.0 / (4 * n_tm)) + water_level)
    second = [remote(inv.at[me], inv.at[me], send2.at[d], recv2.at[me], me_c, tms[d]) for d in range(1, n_tm)]
    for copy in second:
        copy.start()

    for t in range(3, far):
        ring_round(t)

    cross = [remote(keep.at[k], crossed.at[k], cross_send.at[k], cross_recv.at[k], partner, me) for k in range(STEPS)]
    for k in range(STEPS):
        total = None
        for s in range(PARTS):
            for w in range(2):
                hop(w, reach[w][k] - 1, k, s).wait_recv()
            for n in range(s * per, (s + 1) * per):
                value = jnp.where(ahead[k] <= reach[0][k], relayed[0, reach[0][k] - 1, k, n],
                                  relayed[1, reach[1][k] - 1, k, n])
                value = jnp.where(ahead[k] == 0, own(k, n, z), value)
                keep[k, n] = value
                value = value.astype(f32)
                total = value * value if total is None else total + value * value
        cross[k].start()
        ppart[k * half:(k + 1) * half] = total.astype(bf16)
    spot = hi * n_tm + me
    third = [remote(ppart, pgot.at[spot], send3.at[i], recv3.at[spot], chan, tm)
             for i, (chan, _, tm) in enumerate(group)]
    for copy in third[::-1]:
        copy.start()

    def whiten(p):
        factor = inv[p]
        for n in range(8):
            at = pl.ds(pl.multiple_of(n * freq + p * cols, cols), cols)
            value = (x_ref[:, at].astype(f32) * factor).astype(bf16)
            w2[:rows, at] = value
            w2[rows:, at] = value

    whiten(me)
    for d in range(1, n_tm):
        remote(inv.at[me], inv.at[back[d]], send2.at[d], recv2.at[back[d]], me_c, tms[d]).wait_recv()
        whiten(back[d])

    def receiver_features(i, _):
        for r in range(0, rows, 16):
            x = [w2[r:r + 16, pl.ds(pl.multiple_of(n * freq + i * 128, 128), 128)].astype(f32) for n in range(8)]

            def out(n, value):
                value = value.astype(bf16)
                fr[i, r:r + 16, n * 128:(n + 1) * 128] = value
                fr[i, rows + r:rows + r + 16, n * 128:(n + 1) * 128] = value

            features(x, out, True)
        return 0

    sums = [ppart[...].astype(f32), jnp.zeros(ppart.shape, f32)]
    for i, ((chan, _, tm), (h, t)) in enumerate(zip(group, group_back)):
        other = h * n_tm + t
        remote(ppart, pgot.at[other], send3.at[i], recv3.at[other], chan, tm).wait_recv()
        side = 0 if i < n_tm - 1 else 1
        sums[side] = sums[side] + pgot[other].astype(f32)
    for k in range(STEPS):
        from_here = lax.rem(blocks[k] // 2, 2) == hi
        at = slice(k * half, (k + 1) * half)
        total = jnp.where(from_here, sums[0][at], sums[1][at])
        factor = 1.0 / jnp.sqrt(total * (1.0 / (4 * n_tm)) + water_level)
        cross[k].wait()
        for n in range(8):
            value = jnp.where(from_here, keep[k, n], crossed[k, n])
            pieces[core, z, k, n] = (value.astype(f32) * factor).astype(bf16)

    def around(w, t, k, s, arriving):
        d = t + 1 if arriving else t
        ref = pieces.at[core, above(-d) if w == 0 else above(d), k, pl.ds(s * per, per)]
        return remote(ref, ref, around_send.at[w, t, k * PARTS + s], around_recv.at[w, t, k * PARTS + s], ways[w], me)

    def pass_over(d, c):
        ref = pieces.at[c, above(d)]
        slot = d + n_z // 2
        return remote(ref, ref, pass_send.at[slot], pass_recv.at[slot], sibling, me)

    def add_energy(d, energy):
        plane = above(d)
        for c in (core, 1 - core):
            if c is not core:
                pass_over(d, 1 - core).wait_recv()
            for k in range(STEPS):
                for q in range(2):
                    at = pl.ds(pl.multiple_of(k * SRC + c * half + q * 16, 16), 16)
                    x = [pieces[c, plane, k, n, q * 16:q * 16 + 16, :].astype(f32) for n in range(8)]
                    for n in range(8):
                        s32[plane, n, at, :] = x[n]

                    def out(n, value):
                        fs[at, n * 128:(n + 1) * 128] = value.astype(bf16)

                    features(x, out, False)
        return energy + lax.dot_general(fs[...], fr[plane], (((1,), (1,)), ((), ())), preferred_element_type=f32)

    for k, s in subs:
        for w in range(2):
            around(w, 0, k, s, False).start()
        if (k, s) == subs[0]:
            pass_over(0, core).start()
        at = subs.index((k, s))
        lax.fori_loop(at * n_z // len(subs), (at + 1) * n_z // len(subs), receiver_features, 0)
    energy = jnp.zeros((STEPS * SRC, 2 * rows), f32)
    for t in range(1, far + 1):
        if t == far:
            energy = add_energy(1 - t, energy)
            energy = add_energy(t - 1, energy)
        for k, s in subs:
            for w in range(2):
                if t <= reach[w][k]:
                    around(w, t - 1, k, s, True).wait_recv()
                if t < reach[w][k]:
                    around(w, t, k, s, False).start()
        pass_over(-t, core).start()
        if t < far:
            pass_over(t, core).start()
            energy = add_energy(1 - t, energy)
            if t > 1:
                energy = add_energy(t - 1, energy)
    energy = add_energy(-far, energy)
    scale = lax.rsqrt(jnp.maximum(energy, 0.0) * (1.0 / (2 * freq)) + pair_eps)

    def weigh(step):
        weight = scale[step * SRC:(step + 1) * SRC]
        slot = slots[step]
        for k in range(SLOTS):
            value = jnp.where(slot == float(k), weight, 0.0)
            high = value.astype(bf16).astype(f32)
            amat[step, k * SRC:(k + 1) * SRC, :] = jnp.where(lane < rows, high, value - high).astype(bf16)

    def project(step, chunk, wf, t):
        for n in range(8):
            wf[:, n * 128:(n + 1) * 128] = w2[:, pl.ds(pl.multiple_of(n * freq + chunk * 128, 128), 128)]
        t[...] = jnp.dot(amat[step], wf[...], preferred_element_type=f32)

    def gather(step, chunk, t):
        for k in range(SLOTS):
            sums = [None] * 4
            for g in range(SRC // 8):
                r = k * SRC + g * 8
                row = step * SRC + g * 8
                re, im = [], []
                for a in range(4):
                    tr = t[r:r + 8, 2 * a * 128:(2 * a + 1) * 128]
                    ti = t[r:r + 8, (2 * a + 1) * 128:(2 * a + 2) * 128]
                    sr = s32[chunk, 2 * a, row:row + 8, :]
                    si = s32[chunk, 2 * a + 1, row:row + 8, :]
                    re += [sr * tr, si * ti]
                    im.append(sr * ti - si * tr)
                real = ((re[0] + re[1]) + (re[2] + re[3])) + ((re[4] + re[5]) + (re[6] + re[7]))
                imag = (im[0] + im[1]) + (im[2] + im[3])
                mark = hmask[step, r:r + 8, :]
                new = [real, imag, real * mark, imag * mark]
                sums = new if g == 0 else [x + y for x, y in zip(sums, new)]
            for n in range(2):
                base = n * SLOTS * 8 + k * 8
                acc[step, base:base + 8, :128] = sums[2 * n]
                acc[step, base:base + 8, 128:] = sums[2 * n + 1]

    def swap(p):
        return remote(out0.at[p], got0.at[p], swap_send.at[p], swap_recv.at[p], sibling, me)

    def to_owner(p, h):
        return remote(out1.at[p, h], got1.at[spot], send4.at[p, h], recv4.at[spot], z * 4 + h * 2 + core, p)

    def to_owners(p, act):
        for h in range(2):
            @pl.when((p != me) | (hi != h))
            def _():
                act(to_owner(p, h))

    def by_chip(value):
        value = value.reshape(n_z, 2, 8, cols)
        return [value[:, h].reshape(bins // 2, cols).astype(bf16) for h in range(2)]

    def hand_on(p):
        swap(p).wait_recv()
        out1[p, 0], out1[p, 1] = by_chip(mine[p] + got0[p].astype(f32))
        to_owners(p, lambda copy: copy.start())

    def chunk(q):
        return lax.rem(me + 1 + q, n_tm)

    weigh(0)
    project(0, chunk(0), wf0, t0)
    weigh(1)

    def one_chunk(q, _):
        p = chunk(q)
        project(1, p, wf1, t1)
        gather(0, p, t0)
        project(0, chunk(q + 1), wf0, t0)
        gather(1, p, t1)
        rows_of = []
        for step in range(STEPS):
            value = jnp.sum(acc[step].reshape(span, 8, 256), axis=1)
            high = value.astype(bf16).astype(f32)
            rows_of += [high, value - high]
        out = jnp.dot(place[...], jnp.concatenate(rows_of, 0).astype(bf16), preferred_element_type=f32)
        mine[p] = jnp.where(core == 0, out[:, :128], out[:, 128:])
        out0[p] = jnp.where(core == 0, out[:, 128:], out[:, :128]).astype(bf16)

        @pl.when(q < n_tm - 1)
        def _():
            swap(p).start()

        @pl.when(q > 0)
        def _():
            hand_on(chunk(q - 1))

        return 0

    lax.fori_loop(0, n_tm, one_chunk, 0)
    out1[me, 0], out1[me, 1] = by_chip(mine[me])
    to_owners(me, lambda copy: copy.start())
    last_out[0], last_out[1] = by_chip(out0[me].astype(f32))

    def last(i, h, chan):
        return remote(last_out.at[h], last_got.at[i], last_send.at[i], last_recv.at[i], chan, me)

    lasts = [last(0, hi, sibling), last(1, 1 - hi, across)]
    for copy in lasts[::-1]:
        copy.start()
    total = out1[me, hi].astype(f32)
    for (chan, _, tm), (h, t) in zip(group, group_back):
        other = h * n_tm + t
        remote(out1.at[me, hi], got1.at[other], send4.at[me, hi], recv4.at[other], chan, tm).wait_recv()
        total = total + got1[other].astype(f32)
    for i in range(2):
        lasts[i].wait_recv()
        total = total + last_got[i].astype(f32)
    out2[...] = total.reshape(out2.shape)

    def to_plane(d):
        return remote(out2.at[above(d)], got2.at[z], send5.at[d], recv5.at[z], above(d) * 4 + hi * 2 + core, me)

    for d in sorted(range(1, n_z), key=lambda d: -min(d, n_z - d)):
        to_plane(d).start()
    total = out2[z]
    for d in range(1, n_z):
        other = above(-d)
        remote(out2.at[z], got2.at[other], send5.at[d], recv5.at[other], above(d) * 4 + hi * 2 + core, me).wait_recv()
        total = total + got2[other]
    got3[me] = total
    fifth = [remote(got3.at[me], got3.at[me], send6.at[d], recv6.at[me], me_c, tms[d]) for d in range(1, n_tm)]
    for copy in fifth:
        copy.start()
    for d in range(1, n_tm):
        remote(got3.at[me], got3.at[back[d]], send6.at[d], recv6.at[back[d]], me_c, tms[d]).wait_recv()
    for n in range(n_tm):
        value = got3[n]
        high = value.astype(bf16).astype(f32)
        xk[:, n * cols:(n + 1) * cols] = jnp.concatenate([high, value - high], 0).astype(bf16)
    load.wait()
    lag = 512

    def lag_swap(i):
        return remote(lag_out.at[i], lag_got.at[i], lag_send.at[i], lag_recv.at[i], sibling, me)

    for i in range(2 * freq // lag):
        both = jnp.dot(xk[...], table[:, i * lag:(i + 1) * lag], preferred_element_type=f32)
        both = both[:8] + both[8:]
        lag_out[i] = jnp.where(core == 0, both[BIN_DEV:], both[:BIN_DEV])
        lag_swap(i).start()
        out_ref[:, i * lag:(i + 1) * lag] = jnp.where(core == 0, both[:BIN_DEV], both[BIN_DEV:])
    for i in range(2 * freq // lag):
        lag_swap(i).wait_recv()
        at = slice(i * lag, (i + 1) * lag)
        out_ref[:, at] = (out_ref[:, at] + lag_got[i]) * norm

    for w in range(2):
        for k, s in subs:
            for t in range(reach[w][k]):
                hop(w, t, k, s).wait_send()
                around(w, t, k, s, False).wait_send()
    for d in range(-far, far):
        pass_over(d, core).wait_send()
    for p in range(n_tm):
        to_owners(p, lambda copy: copy.wait_send())

        @pl.when(p != me)
        def _():
            swap(p).wait_send()


    for d in range(1, n_z):
        to_plane(d).wait_send()
    for i in range(2 * freq // lag):
        lag_swap(i).wait_send()
    for copy in first + second + third + fifth + lasts:
        copy.wait_send()


def lag_table(freq):
    width = 2 * freq
    phase = np.outer(np.arange(freq), np.arange(width) - freq) % width
    angle = 2.0 * np.pi / width * phase
    return np.concatenate([np.cos(angle), -np.sin(angle)], 0).astype(jnp.bfloat16)


def local(spectra, positions, source_order):
    rows, seg_dev, lags = spectra.shape
    n_chan = lax.axis_size("chan")
    n_tm = lax.axis_size("tm")
    bins = BIN_DEV * n_chan
    pos2 = positions.reshape(n_chan // 2, 2 * rows)
    width = seg_dev * lags
    freq = lags // 2
    cols = freq // n_tm
    n_z = n_chan // 4
    half = rows // 2
    up = n_z // 2
    vm = pl.BlockSpec(memory_space=pltpu.VMEM)
    hbm = pl.BlockSpec(memory_space=pl.ANY)
    dma = pltpu.SemaphoreType.DMA
    vmem = pltpu.VMEM
    return pl.pallas_call(
        functools.partial(kernel, n_chan, n_tm),
        out_shape=jax.ShapeDtypeStruct((BIN_DEV, lags), f32),
        in_specs=[pl.BlockSpec(memory_space=pltpu.SMEM), vm, hbm, hbm],
        out_specs=vm,
        scratch_shapes=[
            vmem((rows, seg_dev, lags), bf16),
            vmem((rows, width), bf16),
            vmem((half, width), bf16),
            vmem((n_tm, rows, cols), f32),
            vmem((n_tm, rows, cols), f32),
            vmem((n_tm, rows, cols), f32),
            vmem((2, up, STEPS, 8, half, 128), bf16),
            vmem((2, up, STEPS, 8, half, 128), bf16),
            vmem((STEPS, 8, half, 128), bf16),
            vmem((STEPS, 8, half, 128), bf16),
            vmem((STEPS * half, 128), bf16),
            vmem((2 * n_tm, STEPS * half, 128), bf16),
            vmem((2, n_z, STEPS, 8, half, 128), bf16),
            vmem((2 * rows, width), bf16),
            vmem((n_z, 8, STEPS * SRC, 128), f32),
            vmem((STEPS * SRC, 16 * 128), bf16),
            vmem((n_z, 2 * rows, 16 * 128), bf16),
            vmem((STEPS, SRC, 2 * rows), f32),
            vmem((STEPS, SLOTS * SRC, 2 * rows), bf16),
            vmem((STEPS, SLOTS * SRC, 128), f32),
            vmem((2 * rows, 1024), bf16),
            vmem((2 * rows, 1024), bf16),
            vmem((SLOTS * SRC, 1024), f32),
            vmem((SLOTS * SRC, 1024), f32),
            vmem((STEPS, 2 * SLOTS * 8, 256), f32),
            vmem((bins, 4 * STEPS * SLOTS), bf16),
            vmem((freq, lags), bf16),
            vmem((n_tm, bins, cols), f32),
            vmem((n_tm, bins, cols), bf16),
            vmem((n_tm, bins, cols), bf16),
            vmem((n_tm, 2, bins // 2, cols), bf16),
            vmem((2 * n_tm, bins // 2, cols), bf16),
            vmem((2, bins // 2, cols), bf16),
            vmem((2, bins // 2, cols), bf16),
            vmem((n_z, bins // n_z // 2, cols), f32),
            vmem((n_z, bins // n_z // 2, cols), f32),
            vmem((n_tm, bins // n_z // 2, cols), f32),
            vmem((16, freq), bf16),
            vmem((4, BIN_DEV, lags // 4), f32),
            vmem((4, BIN_DEV, lags // 4), f32),
            dma((1,)), dma((1,)), dma((2,)), dma((2,)), dma((n_tm,)), dma((n_tm,)), dma((n_tm,)), dma((n_tm,)),
            dma((2, up, STEPS * PARTS)), dma((2, up, STEPS * PARTS)), dma((2,)), dma((2,)), dma((2 * n_tm,)), dma((2 * n_tm,)),
            dma((2, up, STEPS * PARTS)), dma((2, up, STEPS * PARTS)), dma((n_z,)), dma((n_z,)),
            dma((n_tm,)), dma((n_tm,)), dma((n_tm, 2)), dma((2 * n_tm,)), dma((n_z,)), dma((n_z,)),
            dma((2,)), dma((2,)), dma((n_tm,)), dma((n_tm,)), dma((4,)), dma((4,)),
        ],
        compiler_params=pltpu.CompilerParams(collective_id=0, has_side_effects=True, vmem_limit_bytes=58 * MIB),
        name="offset_stack",
    )(source_order, pos2, spectra, jnp.asarray(lag_table(freq)))


def solution(mesh):
    return jax.shard_map(
        local,
        mesh=mesh,
        in_specs=(P("chan", "tm", None), P(), P()),
        out_specs=P("chan", None),
        check_vma=False,
    )
```

```python
import functools

import jax
import jax.numpy as jnp
import numpy as np
from jax import lax
from jax.experimental import pallas as pl
from jax.experimental.pallas import tpu as pltpu
from jax.sharding import PartitionSpec as P

SRC = 64
STEPS = 2
SLOTS = 12
BIN_DEV = 4
PARTS = 2
MIB = 1024 * 1024

water_level = 0.1
pair_eps = 1e-06
f32 = jnp.float32
bf16 = jnp.bfloat16


def to_bins(gap, loop, bins):
    offset = jnp.minimum(gap, loop - gap)
    return jnp.floor((offset * (2 * bins) + 0.5) * (1.0 / (loop + 1)))


def block_column(pos_ref, block):
    row = pos_ref[pl.ds(block // 2, 1), :].astype(f32)
    shape = (SRC, 2 * SRC)
    from_lane = lax.broadcasted_iota(jnp.int32, shape, 1) - lax.broadcasted_iota(jnp.int32, shape, 0)
    return jnp.sum(jnp.where(from_lane == lax.rem(block, 2) * SRC, row, 0.0), axis=1, keepdims=True)


def features(x, out, double):
    re, im = x[0::2], x[1::2]
    n = 0
    for a in range(4):
        out(n, re[a] * re[a] + im[a] * im[a])
        n += 1
    for a in range(4):
        for b in range(a + 1, 4):
            real = re[a] * re[b] + im[a] * im[b]
            imag = re[a] * im[b] - im[a] * re[b]
            if double:
                real, imag = real + real, imag + imag
            out(n, real)
            out(n + 1, imag)
            n += 2


def kernel(n_chan, n_tm, order_ref, pos_ref, spectra_ref, table_ref, out_ref,
           raw, x_ref, sib, part, got, inv, relay, relayed, keep, crossed, ppart, pgot, pieces,
           w2, s32, fs, fr, slots, amat, hmask, wf0, wf1, t0, t1, acc,
           place, table, mine, out0, got0, out1, got1, last_out, last_got, out2, got2, got3, xk, lag_out, lag_got,
           table_sem, raw_sem, share_send, share_recv, send1, recv1, send2, recv2, ring_send, ring_recv, cross_send, cross_recv,
           send3, recv3, around_send, around_recv, pass_send, pass_recv,
           swap_send, swap_recv, send4, recv4, send5, recv5, last_send, last_recv, send6, recv6, lag_send, lag_recv):
    rows, width = x_ref.shape
    freq = width // 8
    cols = freq // n_tm
    half = rows // 2
    bins = BIN_DEV * n_chan
    channels = n_chan * rows
    loop = float(channels + 1 + (channels - 1) // 2)
    me_c, me = lax.axis_index("chan"), lax.axis_index("tm")
    n_z = n_chan // 4
    zh, core = me_c // 2, lax.rem(me_c, 2)
    z, hi = zh // 2, lax.rem(zh, 2)
    sibling, partner = zh * 2 + 1 - core, z * 4 + (1 - hi) * 2 + core

    def above(d):
        return lax.rem(z + d + n_z, n_z)

    ways = [above(1) * 4 + hi * 2 + core, above(-1) * 4 + hi * 2 + core]
    far = n_z // 2
    reach = [[far - (w != k) for k in range(STEPS)] for w in range(2)]
    tms = [lax.rem(me + d, n_tm) for d in range(n_tm)]
    back = [lax.rem(me - d + n_tm, n_tm) for d in range(n_tm)]
    group = [(me_c, hi, tms[d]) for d in range(1, n_tm)] + [(partner, 1 - hi, tms[d]) for d in range(n_tm)]
    group_back = [(hi, back[d]) for d in range(1, n_tm)] + [(1 - hi, back[d]) for d in range(n_tm)]

    barrier = pltpu.get_barrier_semaphore()
    for chan, _, tm in group:
        pl.semaphore_signal(barrier, inc=1, device_id={"chan": chan, "tm": tm})
    across = z * 4 + (1 - hi) * 2 + 1 - core
    for chan in (sibling, across):
        pl.semaphore_signal(barrier, inc=1, device_id={"chan": chan, "tm": me})
    for d in range(1, n_z):
        pl.semaphore_signal(barrier, inc=1, device_id={"chan": above(d) * 4 + hi * 2 + core, "tm": me})
    load = pltpu.make_async_copy(table_ref.at[pl.ds(pl.multiple_of(core * freq, freq), freq)], table, table_sem.at[0])
    fetch = pltpu.make_async_copy(spectra_ref, raw, raw_sem.at[0])
    fetch.start()
    fetch.wait()
    load.start()
    lags = raw.shape[2]
    for a in range(raw.shape[1]):
        x_ref[:, a * lags:(a + 1) * lags] = raw[:, a, :]
    pl.semaphore_wait(barrier, len(group) + n_z + 1)

    def remote(src, dst, send, recv, chan, tm):
        return pltpu.make_async_remote_copy(src_ref=src, dst_ref=dst, send_sem=send, recv_sem=recv,
                                            device_id={"chan": chan, "tm": tm})

    def share(s):
        at = pl.ds(s * 4 * freq, 4 * freq)
        return remote(x_ref.at[pl.ds(pl.multiple_of((1 - core) * half, half), half), at], sib.at[:, at],
                      share_send.at[s], share_recv.at[s], sibling, me)

    share(0).start()
    blocks = [order_ref[k] for k in range(STEPS)]
    ahead = [lax.rem(z - blocks[k] // 4 + n_z, n_z) for k in range(STEPS)]
    own_core = [lax.rem(blocks[k], 2) == core for k in range(STEPS)]
    mine_at = pl.ds(pl.multiple_of(core * half, half), half)
    subs = [(k, s) for s in range(PARTS) for k in range(STEPS)]
    per = 8 // PARTS

    def own(k, n, plane):
        at = pl.ds(pl.multiple_of(n * freq + plane * 128, 128), 128)
        return jnp.where(own_core[k], x_ref[mine_at, at], sib[:, at])

    def hop(w, t, k, s):
        n = pl.ds(s * per, per)
        return remote(relay.at[w, t, k, n], relayed.at[w, t, k, n], ring_send.at[w, t, k * PARTS + s],
                      ring_recv.at[w, t, k * PARTS + s], ways[w], me)

    def ring_round(t, between=()):
        for k, s in subs:
            if t == 0 and k == 0 and s % (PARTS // 2) == 0:
                share(s // (PARTS // 2)).wait()
                if s == 0:
                    share(1).start()
            for w in range(2):
                if t >= reach[w][k]:
                    continue
                plane = above(reach[w][k] - t) if w == 0 else above(t - reach[w][k])
                if t:
                    hop(w, t - 1, k, s).wait_recv()
                for n in range(s * per, (s + 1) * per):
                    value = own(k, n, plane)
                    if t:
                        value = jnp.where(ahead[k] == 0, value, relayed[w, t - 1, k, n])
                    relay[w, t, k, n] = value
                hop(w, t, k, s).start()
            if between:
                between.pop(0)()

    def power(first_p, last_p):
        for p in range(first_p, last_p):
            total = None
            for n in range(8):
                v = x_ref[:, n * freq + p * cols:n * freq + (p + 1) * cols].astype(f32)
                total = v * v if total is None else total + v * v
            part[p] = total

    first = [remote(part.at[tms[d]], got.at[me], send1.at[d], recv1.at[me], me_c, tms[d]) for d in range(1, n_tm)]

    counts = []

    def count_pairs(k):
        src = block_column(pos_ref, blocks[k])

        def count(i, sums):
            pair_bins = to_bins(jnp.abs(src - pos_ref[pl.ds(i, 1), :].astype(f32)), loop, bins)
            rel = pair_bins - (me_c * BIN_DEV).astype(f32)
            return tuple(s + jnp.where(rel == float(b), 1.0, 0.0) for b, s in enumerate(sums))

        init = tuple(jnp.zeros((SRC, pos_ref.shape[1]), f32) for _ in range(BIN_DEV))
        counts.append(lax.fori_loop(0, pos_ref.shape[0], count, init))

    step = n_tm // len(subs)
    ring_round(0, [functools.partial(power, i * step, (i + 1) * step) for i in range(len(subs))])
    for copy in first:
        copy.start()
    for k in range(STEPS):
        count_pairs(k)
    factors = []
    for b in range(BIN_DEV):
        amount = sum(c[b] for c in counts)
        amount = jnp.sum(jnp.sum(amount, axis=1, keepdims=True), axis=0, keepdims=True)
        alone = jnp.where(me_c * BIN_DEV + b == 0, float(STEPS * SRC), 0.0)
        factors.append(lax.rsqrt((amount - alone) * float(n_tm * freq)))
    norm = jnp.concatenate(factors, 0)

    ring_round(1)

    lane = lax.broadcasted_iota(jnp.int32, (SRC, 2 * rows), 1)
    rec = pos_ref[pl.ds(zh, 1), :].astype(f32)
    rec = jnp.where(lane[:1] // rows == core, rec, pltpu.roll(rec, rows, axis=1))
    rec_ids = me_c * rows + lane % rows
    span = 2 * SLOTS
    col = lax.broadcasted_iota(jnp.int32, (bins, 2 * STEPS * span), 1)
    row = lax.broadcasted_iota(jnp.int32, (bins, 2 * STEPS * span), 0).astype(f32)
    inner = col % span
    marked = inner >= SLOTS
    first_bin = jnp.zeros((1, 1), f32)
    for step in range(STEPS):
        block = blocks[step]
        pair_bins = to_bins(jnp.abs(block_column(pos_ref, block) - rec), loop, bins)
        src_ids = block * SRC + lax.broadcasted_iota(jnp.int32, (SRC, 2 * rows), 0)
        lowest = jnp.min(jnp.min(pair_bins, axis=1, keepdims=True), axis=0, keepdims=True)
        first_bin = jnp.where(col < step * 2 * span, first_bin, lowest)
        rel = pair_bins - lowest
        upper = rel >= float(SLOTS)
        slot = jnp.where(upper, rel - float(SLOTS), rel)
        slots[step] = jnp.where(src_ids == rec_ids, -1.0, slot)
        for k in range(SLOTS):
            mark = jnp.max(jnp.where((slot == float(k)) & upper, 1.0, 0.0), axis=1, keepdims=True)
            hmask[step, k * SRC:(k + 1) * SRC, :] = jnp.broadcast_to(mark, (SRC, 128))
    at = first_bin + (inner - jnp.where(marked, SLOTS, 0)).astype(f32)
    lower = jnp.where(row == at, 1.0, 0.0)
    place[...] = jnp.where(marked, jnp.where(row == at + float(SLOTS), 1.0, 0.0) - lower, lower).astype(bf16)

    ring_round(2)

    total = part[me]
    for d in range(1, n_tm):
        remote(part.at[me], got.at[back[d]], send1.at[d], recv1.at[back[d]], me_c, tms[d]).wait_recv()
        total = total + got[back[d]]
    inv[me] = 1.0 / jnp.sqrt(total * (1.0 / (4 * n_tm)) + water_level)
    second = [remote(inv.at[me], inv.at[me], send2.at[d], recv2.at[me], me_c, tms[d]) for d in range(1, n_tm)]
    for copy in second:
        copy.start()

    for t in range(3, far):
        ring_round(t)

    cross = [remote(keep.at[k], crossed.at[k], cross_send.at[k], cross_recv.at[k], partner, me) for k in range(STEPS)]
    for k in range(STEPS):
        total = None
        for s in range(PARTS):
            for w in range(2):
                hop(w, reach[w][k] - 1, k, s).wait_recv()
            for n in range(s * per, (s + 1) * per):
                value = jnp.where(ahead[k] <= reach[0][k], relayed[0, reach[0][k] - 1, k, n],
                                  relayed[1, reach[1][k] - 1, k, n])
                value = jnp.where(ahead[k] == 0, own(k, n, z), value)
                keep[k, n] = value
                value = value.astype(f32)
                total = value * value if total is None else total + value * value
        cross[k].start()
        ppart[k * half:(k + 1) * half] = total.astype(bf16)
    spot = hi * n_tm + me
    third = [remote(ppart, pgot.at[spot], send3.at[i], recv3.at[spot], chan, tm)
             for i, (chan, _, tm) in enumerate(group)]
    for copy in third[::-1]:
        copy.start()

    def whiten(p):
        factor = inv[p]
        for n in range(8):
            at = pl.ds(pl.multiple_of(n * freq + p * cols, cols), cols)
            value = (x_ref[:, at].astype(f32) * factor).astype(bf16)
            w2[:rows, at] = value
            w2[rows:, at] = value

    whiten(me)
    for d in range(1, n_tm):
        remote(inv.at[me], inv.at[back[d]], send2.at[d], recv2.at[back[d]], me_c, tms[d]).wait_recv()
        whiten(back[d])

    def receiver_features(i, _):
        for r in range(0, rows, 16):
            x = [w2[r:r + 16, pl.ds(pl.multiple_of(n * freq + i * 128, 128), 128)].astype(f32) for n in range(8)]

            def out(n, value):
                value = value.astype(bf16)
                fr[i, r:r + 16, n * 128:(n + 1) * 128] = value
                fr[i, rows + r:rows + r + 16, n * 128:(n + 1) * 128] = value

            features(x, out, True)
        return 0

    sums = [ppart[...].astype(f32), jnp.zeros(ppart.shape, f32)]
    for i, ((chan, _, tm), (h, t)) in enumerate(zip(group, group_back)):
        other = h * n_tm + t
        remote(ppart, pgot.at[other], send3.at[i], recv3.at[other], chan, tm).wait_recv()
        side = 0 if i < n_tm - 1 else 1
        sums[side] = sums[side] + pgot[other].astype(f32)
    for k in range(STEPS):
        from_here = lax.rem(blocks[k] // 2, 2) == hi
        at = slice(k * half, (k + 1) * half)
        total = jnp.where(from_here, sums[0][at], sums[1][at])
        factor = 1.0 / jnp.sqrt(total * (1.0 / (4 * n_tm)) + water_level)
        cross[k].wait()
        for n in range(8):
            value = jnp.where(from_here, keep[k, n], crossed[k, n])
            pieces[core, z, k, n] = (value.astype(f32) * factor).astype(bf16)

    def around(w, t, k, s, arriving):
        d = t + 1 if arriving else t
        ref = pieces.at[core, above(-d) if w == 0 else above(d), k, pl.ds(s * per, per)]
        return remote(ref, ref, around_send.at[w, t, k * PARTS + s], around_recv.at[w, t, k * PARTS + s], ways[w], me)

    def pass_over(d, c):
        ref = pieces.at[c, above(d)]
        slot = d + n_z // 2
        return remote(ref, ref, pass_send.at[slot], pass_recv.at[slot], sibling, me)

    def add_energy(d, energy):
        plane = above(d)
        for c in (core, 1 - core):
            if c is not core:
                pass_over(d, 1 - core).wait_recv()
            for k in range(STEPS):
                for q in range(2):
                    at = pl.ds(pl.multiple_of(k * SRC + c * half + q * 16, 16), 16)
                    x = [pieces[c, plane, k, n, q * 16:q * 16 + 16, :].astype(f32) for n in range(8)]
                    for n in range(8):
                        s32[plane, n, at, :] = x[n]

                    def out(n, value):
                        fs[at, n * 128:(n + 1) * 128] = value.astype(bf16)

                    features(x, out, False)
        return energy + lax.dot_general(fs[...], fr[plane], (((1,), (1,)), ((), ())), preferred_element_type=f32)

    for k, s in subs:
        for w in range(2):
            around(w, 0, k, s, False).start()
        if (k, s) == subs[0]:
            pass_over(0, core).start()
        at = subs.index((k, s))
        lax.fori_loop(at * n_z // len(subs), (at + 1) * n_z // len(subs), receiver_features, 0)
    energy = jnp.zeros((STEPS * SRC, 2 * rows), f32)
    for t in range(1, far + 1):
        if t == far:
            energy = add_energy(1 - t, energy)
            energy = add_energy(t - 1, energy)
        for k, s in subs:
            for w in range(2):
                if t <= reach[w][k]:
                    around(w, t - 1, k, s, True).wait_recv()
                if t < reach[w][k]:
                    around(w, t, k, s, False).start()
        pass_over(-t, core).start()
        if t < far:
            pass_over(t, core).start()
            energy = add_energy(1 - t, energy)
            if t > 1:
                energy = add_energy(t - 1, energy)
    energy = add_energy(-far, energy)
    scale = lax.rsqrt(jnp.maximum(energy, 0.0) * (1.0 / (2 * freq)) + pair_eps)

    def weigh(step):
        weight = scale[step * SRC:(step + 1) * SRC]
        slot = slots[step]
        for k in range(SLOTS):
            value = jnp.where(slot == float(k), weight, 0.0)
            high = value.astype(bf16).astype(f32)
            amat[step, k * SRC:(k + 1) * SRC, :] = jnp.where(lane < rows, high, value - high).astype(bf16)

    def project(step, chunk, wf, t):
        for n in range(8):
            wf[:, n * 128:(n + 1) * 128] = w2[:, pl.ds(pl.multiple_of(n * freq + chunk * 128, 128), 128)]
        t[...] = jnp.dot(amat[step], wf[...], preferred_element_type=f32)

    def gather(step, chunk, t):
        for k in range(SLOTS):
            sums = [None] * 4
            for g in range(SRC // 8):
                r = k * SRC + g * 8
                row = step * SRC + g * 8
                re, im = [], []
                for a in range(4):
                    tr = t[r:r + 8, 2 * a * 128:(2 * a + 1) * 128]
                    ti = t[r:r + 8, (2 * a + 1) * 128:(2 * a + 2) * 128]
                    sr = s32[chunk, 2 * a, row:row + 8, :]
                    si = s32[chunk, 2 * a + 1, row:row + 8, :]
                    re += [sr * tr, si * ti]
                    im.append(sr * ti - si * tr)
                real = ((re[0] + re[1]) + (re[2] + re[3])) + ((re[4] + re[5]) + (re[6] + re[7]))
                imag = (im[0] + im[1]) + (im[2] + im[3])
                mark = hmask[step, r:r + 8, :]
                new = [real, imag, real * mark, imag * mark]
                sums = new if g == 0 else [x + y for x, y in zip(sums, new)]
            for n in range(2):
                base = n * SLOTS * 8 + k * 8
                acc[step, base:base + 8, :128] = sums[2 * n]
                acc[step, base:base + 8, 128:] = sums[2 * n + 1]

    def swap(p):
        return remote(out0.at[p], got0.at[p], swap_send.at[p], swap_recv.at[p], sibling, me)

    def to_owner(p, h):
        return remote(out1.at[p, h], got1.at[spot], send4.at[p, h], recv4.at[spot], z * 4 + h * 2 + core, p)

    def to_owners(p, act):
        for h in range(2):
            @pl.when((p != me) | (hi != h))
            def _():
                act(to_owner(p, h))

    def by_chip(value):
        value = value.reshape(n_z, 2, 8, cols)
        return [value[:, h].reshape(bins // 2, cols).astype(bf16) for h in range(2)]

    def hand_on(p):
        swap(p).wait_recv()
        out1[p, 0], out1[p, 1] = by_chip(mine[p] + got0[p].astype(f32))
        to_owners(p, lambda copy: copy.start())

    def chunk(q):
        return lax.rem(me + 1 + q, n_tm)

    weigh(0)
    project(0, chunk(0), wf0, t0)
    weigh(1)

    def one_chunk(q, _, last_one=False):
        p = chunk(q)
        project(1, p, wf1, t1)
        gather(0, p, t0)
        if not last_one:
            project(0, chunk(q + 1), wf0, t0)
        gather(1, p, t1)
        if last_one:
            hand_on(chunk(q - 1))
        rows_of = []
        for step in range(STEPS):
            value = jnp.sum(acc[step].reshape(span, 8, 256), axis=1)
            high = value.astype(bf16).astype(f32)
            rows_of += [high, value - high]
        out = jnp.dot(place[...], jnp.concatenate(rows_of, 0).astype(bf16), preferred_element_type=f32)
        mine[p] = jnp.where(core == 0, out[:, :128], out[:, 128:])
        out0[p] = jnp.where(core == 0, out[:, 128:], out[:, :128]).astype(bf16)
        if last_one:
            return 0
        swap(p).start()

        @pl.when(q > 0)
        def _():
            hand_on(chunk(q - 1))

        return 0

    lax.fori_loop(0, n_tm - 1, one_chunk, 0)
    one_chunk(n_tm - 1, 0, True)
    out1[me, 0], out1[me, 1] = by_chip(mine[me])
    to_owners(me, lambda copy: copy.start())
    last_out[0], last_out[1] = by_chip(out0[me].astype(f32))

    def last(i, h, chan):
        return remote(last_out.at[h], last_got.at[i], last_send.at[i], last_recv.at[i], chan, me)

    lasts = [last(0, hi, sibling), last(1, 1 - hi, across)]
    for copy in lasts[::-1]:
        copy.start()
    total = out1[me, hi].astype(f32)
    for (chan, _, tm), (h, t) in zip(group, group_back):
        other = h * n_tm + t
        remote(out1.at[me, hi], got1.at[other], send4.at[me, hi], recv4.at[other], chan, tm).wait_recv()
        total = total + got1[other].astype(f32)
    for i in range(2):
        lasts[i].wait_recv()
        total = total + last_got[i].astype(f32)
    out2[...] = total.reshape(out2.shape)

    def to_plane(d):
        return remote(out2.at[above(d)], got2.at[z], send5.at[d], recv5.at[z], above(d) * 4 + hi * 2 + core, me)

    for d in sorted(range(1, n_z), key=lambda d: -min(d, n_z - d)):
        to_plane(d).start()
    total = out2[z]
    for d in range(1, n_z):
        other = above(-d)
        remote(out2.at[z], got2.at[other], send5.at[d], recv5.at[other], above(d) * 4 + hi * 2 + core, me).wait_recv()
        total = total + got2[other]
    got3[me] = total
    fifth = [remote(got3.at[me], got3.at[me], send6.at[d], recv6.at[me], me_c, tms[d]) for d in range(1, n_tm)]
    for copy in fifth:
        copy.start()
    for d in range(1, n_tm):
        remote(got3.at[me], got3.at[back[d]], send6.at[d], recv6.at[back[d]], me_c, tms[d]).wait_recv()
    for n in range(n_tm):
        value = got3[n]
        high = value.astype(bf16).astype(f32)
        xk[:, n * cols:(n + 1) * cols] = jnp.concatenate([high, value - high], 0).astype(bf16)
    load.wait()
    lag = 512

    def lag_swap(i):
        return remote(lag_out.at[i], lag_got.at[i], lag_send.at[i], lag_recv.at[i], sibling, me)

    for i in range(2 * freq // lag):
        both = jnp.dot(xk[...], table[:, i * lag:(i + 1) * lag], preferred_element_type=f32)
        both = both[:8] + both[8:]
        lag_out[i] = jnp.where(core == 0, both[BIN_DEV:], both[:BIN_DEV])
        lag_swap(i).start()
        out_ref[:, i * lag:(i + 1) * lag] = jnp.where(core == 0, both[:BIN_DEV], both[BIN_DEV:])
    for i in range(2 * freq // lag):
        lag_swap(i).wait_recv()
        at = slice(i * lag, (i + 1) * lag)
        out_ref[:, at] = (out_ref[:, at] + lag_got[i]) * norm

    for w in range(2):
        for k, s in subs:
            for t in range(reach[w][k]):
                hop(w, t, k, s).wait_send()
                around(w, t, k, s, False).wait_send()
    for d in range(-far, far):
        pass_over(d, core).wait_send()
    for p in range(n_tm):
        to_owners(p, lambda copy: copy.wait_send())

        @pl.when(p != me)
        def _():
            swap(p).wait_send()


    for d in range(1, n_z):
        to_plane(d).wait_send()
    for i in range(2 * freq // lag):
        lag_swap(i).wait_send()
    for copy in first + second + third + fifth + lasts:
        copy.wait_send()


def lag_table(freq):
    width = 2 * freq
    phase = np.outer(np.arange(freq), np.arange(width) - freq) % width
    angle = 2.0 * np.pi / width * phase
    return np.concatenate([np.cos(angle), -np.sin(angle)], 0).astype(jnp.bfloat16)


def local(spectra, positions, source_order):
    rows, seg_dev, lags = spectra.shape
    n_chan = lax.axis_size("chan")
    n_tm = lax.axis_size("tm")
    bins = BIN_DEV * n_chan
    pos2 = positions.reshape(n_chan // 2, 2 * rows)
    width = seg_dev * lags
    freq = lags // 2
    cols = freq // n_tm
    n_z = n_chan // 4
    half = rows // 2
    up = n_z // 2
    vm = pl.BlockSpec(memory_space=pltpu.VMEM)
    hbm = pl.BlockSpec(memory_space=pl.ANY)
    dma = pltpu.SemaphoreType.DMA
    vmem = pltpu.VMEM
    return pl.pallas_call(
        functools.partial(kernel, n_chan, n_tm),
        out_shape=jax.ShapeDtypeStruct((BIN_DEV, lags), f32),
        in_specs=[pl.BlockSpec(memory_space=pltpu.SMEM), vm, hbm, hbm],
        out_specs=vm,
        scratch_shapes=[
            vmem((rows, seg_dev, lags), bf16),
            vmem((rows, width), bf16),
            vmem((half, width), bf16),
            vmem((n_tm, rows, cols), f32),
            vmem((n_tm, rows, cols), f32),
            vmem((n_tm, rows, cols), f32),
            vmem((2, up, STEPS, 8, half, 128), bf16),
            vmem((2, up, STEPS, 8, half, 128), bf16),
            vmem((STEPS, 8, half, 128), bf16),
            vmem((STEPS, 8, half, 128), bf16),
            vmem((STEPS * half, 128), bf16),
            vmem((2 * n_tm, STEPS * half, 128), bf16),
            vmem((2, n_z, STEPS, 8, half, 128), bf16),
            vmem((2 * rows, width), bf16),
            vmem((n_z, 8, STEPS * SRC, 128), f32),
            vmem((STEPS * SRC, 16 * 128), bf16),
            vmem((n_z, 2 * rows, 16 * 128), bf16),
            vmem((STEPS, SRC, 2 * rows), f32),
            vmem((STEPS, SLOTS * SRC, 2 * rows), bf16),
            vmem((STEPS, SLOTS * SRC, 128), f32),
            vmem((2 * rows, 1024), bf16),
            vmem((2 * rows, 1024), bf16),
            vmem((SLOTS * SRC, 1024), f32),
            vmem((SLOTS * SRC, 1024), f32),
            vmem((STEPS, 2 * SLOTS * 8, 256), f32),
            vmem((bins, 4 * STEPS * SLOTS), bf16),
            vmem((freq, lags), bf16),
            vmem((n_tm, bins, cols), f32),
            vmem((n_tm, bins, cols), bf16),
            vmem((n_tm, bins, cols), bf16),
            vmem((n_tm, 2, bins // 2, cols), bf16),
            vmem((2 * n_tm, bins // 2, cols), bf16),
            vmem((2, bins // 2, cols), bf16),
            vmem((2, bins // 2, cols), bf16),
            vmem((n_z, bins // n_z // 2, cols), f32),
            vmem((n_z, bins // n_z // 2, cols), f32),
            vmem((n_tm, bins // n_z // 2, cols), f32),
            vmem((16, freq), bf16),
            vmem((4, BIN_DEV, lags // 4), f32),
            vmem((4, BIN_DEV, lags // 4), f32),
            dma((1,)), dma((1,)), dma((2,)), dma((2,)), dma((n_tm,)), dma((n_tm,)), dma((n_tm,)), dma((n_tm,)),
            dma((2, up, STEPS * PARTS)), dma((2, up, STEPS * PARTS)), dma((2,)), dma((2,)), dma((2 * n_tm,)), dma((2 * n_tm,)),
            dma((2, up, STEPS * PARTS)), dma((2, up, STEPS * PARTS)), dma((n_z,)), dma((n_z,)),
            dma((n_tm,)), dma((n_tm,)), dma((n_tm, 2)), dma((2 * n_tm,)), dma((n_z,)), dma((n_z,)),
            dma((2,)), dma((2,)), dma((n_tm,)), dma((n_tm,)), dma((4,)), dma((4,)),
        ],
        compiler_params=pltpu.CompilerParams(collective_id=0, has_side_effects=True, vmem_limit_bytes=58 * MIB),
        name="offset_stack",
    )(source_order, pos2, spectra, jnp.asarray(lag_table(freq)))


def solution(mesh):
    return jax.shard_map(
        local,
        mesh=mesh,
        in_specs=(P("chan", "tm", None), P(), P()),
        out_specs=P("chan", None),
        check_vma=False,
    )
```
